512 devices in a mesh: ctx: 32 (over z, core), head: 16 (over x, y).
Axes of the slice: x: 4, y: 4, z: 16, core: 2. Of those that a mesh axis runs over, the one named last changes fastest.
Arguments:
- tokens_in: bfloat16 [8192, 8192], P('ctx', 'head'), may hold values from -6 to 6
- starts: int32 [8192], P('ctx'), may hold values from 0 to 1, as said below
- log_decay: float32 [128, 8192], P('head', 'ctx'), may hold values from -1 to 0
- b_proj: bfloat16 [8192, 128], P('ctx'), may hold values from -0.5 to 0.5
- c_proj: bfloat16 [8192, 128], P('ctx'), may hold values from -0.5 to 0.5
- out_grad: bfloat16 [8192, 8192], P('ctx', 'head'), may hold values from -1.5 to 1.5
- conv_weight: float32 [4, 8192], P(None, 'head'), may hold values from -3 to 3
- conv_bias: float32 [8192], P('head'), may hold values from -3 to 3
- skip_gain: float32 [128], P('head'), may hold values from 0.5 to 2
Outputs:
- in_grad: float32 [8192, 8192], P('ctx', 'head')
- b_grad: float32 [8192, 128], P(('ctx', 'head'))
- c_grad: float32 [8192, 128], P(('ctx', 'head'))
- decay_grad: float32 [128, 8192], P('head', 'ctx')
The draws below stay inside these ranges and needn't reach their ends.
Inputs may be any that keep to these rules, and one draw needn't show every extreme that they name: starts is 0 at every position after 8192 // 8; it is 1 at one or more positions from 1 through 256.
All inputs are finite; a program needn't handle non-finite values.
Results may differ from the reference program's by a relative error of at most 0.003.
Values may be sent and summed in bfloat16 or wider, within the bound.
A program may use at most 64 MiB of HBM per device.

```python
import jax
import jax.numpy as jnp
from jax import lax

SPACE_HEADS = 128
HEAD_DIM = 64
STATE = 128
TAPS = 4
TOKENS_PER_SHARD = 256
CHANNELS = 8192
PACKED_TOKENS = 8192


def draw_starts(key, part):
    key = jax.random.fold_in(key, 5)
    position = jnp.arange(PACKED_TOKENS)
    early = position <= PACKED_TOKENS // 8
    chosen = (jax.random.randint(key, (PACKED_TOKENS,), 0, TOKENS_PER_SHARD // 2) == 0) & early
    forced_place = jax.random.randint(jax.random.fold_in(key, 11), (), 1, TOKENS_PER_SHARD + 1)
    forced = position == forced_place
    return jnp.where(chosen | forced, 1, 0).astype(jnp.int32)


def draw_log_decay(key, part):
    key = jax.random.fold_in(key, 7)
    random_keys = jax.random.split(key, 7)
    fast_heads = jax.random.randint(random_keys[0], (SPACE_HEADS, 1), 0, 2) == 0
    slow_rate = jax.random.uniform(random_keys[1], (SPACE_HEADS, 1), minval=0.5, maxval=1.5) / PACKED_TOKENS
    fast_rate = jnp.exp(jax.random.uniform(random_keys[2], (SPACE_HEADS, 1), minval=0.0, maxval=1.3862944)) / TOKENS_PER_SHARD
    baseline_decay_rate = jnp.where(fast_heads, fast_rate, slow_rate)
    jitter_amplitude = jax.random.uniform(random_keys[3], (SPACE_HEADS, PACKED_TOKENS), minval=0.5, maxval=1.5)
    block_draw = jax.random.uniform(random_keys[4], (SPACE_HEADS, PACKED_TOKENS // TOKENS_PER_SHARD), minval=0.5, maxval=2.0)
    block_multiplier = jnp.repeat(block_draw, TOKENS_PER_SHARD, axis=1)
    spike_position = jax.random.randint(random_keys[5], (1, PACKED_TOKENS), 0, 16 * TOKENS_PER_SHARD) == 0
    spike_length = jax.random.uniform(random_keys[6], (SPACE_HEADS, PACKED_TOKENS), minval=0.22, maxval=0.6)
    value_entry = -(baseline_decay_rate * jitter_amplitude * block_multiplier) - jnp.where(spike_position, spike_length, 0.0)
    return value_entry.astype(jnp.float32)


def level_of(rng, extent, cuts, low, high):
    def one(axis_at, shards_of):
        heights = jax.random.uniform(jax.random.fold_in(jax.random.fold_in(rng, 6), axis_at), (shards_of,), jnp.float32, low / len(cuts), high / len(cuts))
        return jnp.repeat(jnp.exp(heights), extent[axis_at] // shards_of).reshape((-1,) + (1,) * (len(extent) - axis_at - 1))

    gain = one(*cuts[0])
    for cut in cuts[1:]:
        gain = gain * one(*cut)
    return gain


def bell_draw(stream_key, shape, deviation, reach, shards=(), held_as=jnp.bfloat16):
    gain = level_of(stream_key, shape, shards, -0.22, 0.18) if shards else 1.0
    result = jax.random.normal(stream_key, shape, jnp.float32) * deviation * gain
    return jnp.minimum(jnp.maximum(result, -reach), reach).astype(held_as)


def setup_inputs(seed: int = 0) -> dict:
    key_of = jax.random.split(jax.random.key(seed), 10)
    tokens_in = bell_draw(key_of[0], (PACKED_TOKENS, CHANNELS), 1.0, 6.0, ((0, 32), (1, 16)))
    starts = draw_starts(jax.random.fold_in(key_of[9], 71), 0)
    log_decay = draw_log_decay(jax.random.fold_in(key_of[9], 71), 0)
    b_proj = bell_draw(key_of[3], (PACKED_TOKENS, STATE), STATE ** -0.5, 0.5, ((0, 32),))
    c_proj = bell_draw(key_of[4], (PACKED_TOKENS, STATE), STATE ** -0.5, 0.5, ((0, 32),))
    out_grad = bell_draw(key_of[5], (PACKED_TOKENS, CHANNELS), 0.25, 1.5, ((0, 32), (1, 16)))
    conv_weight = bell_draw(key_of[6], (TAPS, CHANNELS), TAPS ** -0.5, 3.0, ((1, 16),), jnp.float32)
    conv_bias = bell_draw(key_of[7], (CHANNELS,), 0.5, 3.0, ((0, 16),), jnp.float32)
    skip_gain = jnp.clip(0.5 + 1.5 * jax.random.uniform(key_of[8], (SPACE_HEADS,), jnp.float32) ** level_of(key_of[8], (SPACE_HEADS,), ((0, 16),), -0.2, 0.2), 0.5, 2.0)
    return {"tokens_in": tokens_in, "starts": starts, "log_decay": log_decay, "b_proj": b_proj, "c_proj": c_proj, "out_grad": out_grad, "conv_weight": conv_weight, "conv_bias": conv_bias, "skip_gain": skip_gain}


highest = lax.Precision.HIGHEST


def silu_slope(value_entry):
    sigma = jax.nn.sigmoid(value_entry)
    return sigma * (1.0 + value_entry * (1.0 - sigma))


def block_setup(log_block, start_block):
    cum_decay = jnp.cumsum(log_block, axis=1)
    doc_count = jnp.cumsum(start_block).astype(jnp.int32)
    keep_in = (doc_count == 0).astype(jnp.float32)
    keep_out = (doc_count == doc_count[-1]).astype(jnp.float32)
    final_cum = cum_decay[:, -1:]
    weight_in = jnp.exp(cum_decay) * keep_in[None, :]
    weight_out = jnp.exp(final_cum - cum_decay) * keep_out[None, :]
    carry_factor = jnp.exp(final_cum[:, 0]) * keep_in[-1]
    return cum_decay, doc_count, weight_in, weight_out, carry_factor


def block_states(act_rows, grad_rows, b_block, c_block, weight_in, weight_out):
    scaled_b = weight_out[:, :, None] * b_block.astype(jnp.float32)[None, :, :]
    scaled_c = weight_in[:, :, None] * c_block.astype(jnp.float32)[None, :, :]
    state_local = jnp.einsum('htn,thp->hnp', scaled_b, act_rows.astype(jnp.float32), precision=highest)
    adjoint_local = jnp.einsum('htn,thp->hnp', scaled_c, grad_rows.astype(jnp.float32), precision=highest)
    return state_local, adjoint_local


def intra_heads(act_heads, grad_heads, cum_decay, doc_count, scores):
    positions = jnp.arange(scores.shape[0])
    lower = (positions[:, None] >= positions[None, :]) & (doc_count[:, None] == doc_count[None, :])

    def one_head(total, inputs):
        act_head, grad_head, cum_head = inputs
        diff = cum_head[:, None] - cum_head[None, :]
        decay = jnp.where(lower, jnp.exp(jnp.minimum(diff, 0.0)), 0.0)
        mixed = decay * scores
        grad_wide = grad_head.astype(jnp.float32)
        act_grad = lax.dot_general(mixed, grad_wide, (((0,), (0,)), ((), ())), precision=highest)
        inner = lax.dot_general(grad_head, act_head, (((1,), (1,)), ((), ())), preferred_element_type=jnp.float32)
        total = total + decay * inner
        product = mixed * inner
        cum_grad = jnp.sum(product, axis=1) - jnp.sum(product, axis=0)
        return total, (act_grad, cum_grad)

    return lax.scan(one_head, jnp.zeros_like(scores), (act_heads, grad_heads, cum_decay))


def inter_terms(act_rows, grad_rows, b_block, c_block, weight_in, weight_out, carry_factor, state_local, state_in, adjoint_in):
    act_wide = act_rows.astype(jnp.float32)
    grad_wide = grad_rows.astype(jnp.float32)
    from_after = jnp.einsum('tn,hnp->thp', b_block.astype(jnp.float32), adjoint_in, precision=highest)
    from_before = jnp.einsum('tn,hnp->thp', c_block.astype(jnp.float32), state_in, precision=highest)
    act_extra = weight_out.T[:, :, None] * from_after
    cum_extra = weight_in * jnp.sum(from_before * grad_wide, axis=2).T - weight_out * jnp.sum(from_after * act_wide, axis=2).T
    state_out = state_local + carry_factor[:, None, None] * state_in
    end_term = jnp.sum(adjoint_in * state_out, axis=(1, 2))
    is_last = (jnp.arange(weight_in.shape[1]) == weight_in.shape[1] - 1).astype(jnp.float32)
    cum_extra = cum_extra + end_term[:, None] * is_last[None, :]
    b_extra = jnp.einsum('thp,hnp->tn', act_wide * weight_out.T[:, :, None], adjoint_in, precision=highest)
    c_extra = jnp.einsum('thp,hnp->tn', grad_wide * weight_in.T[:, :, None], state_in, precision=highest)
    return act_extra, cum_extra, b_extra, c_extra


def reference(tokens_in, starts, log_decay, b_proj, c_proj, out_grad, conv_weight, conv_bias, skip_gain):
    total_tokens = tokens_in.shape[0]
    starts_count = jnp.cumsum(starts).astype(jnp.int32)
    positions = jnp.arange(total_tokens)
    tokens_wide = tokens_in.astype(jnp.float32)
    pre_act = conv_bias[None, :] + conv_weight[0][None, :] * tokens_wide
    for offset in range(1, TAPS):
        earlier_count = jnp.concatenate([jnp.zeros((offset,), jnp.int32), starts_count[:-offset]])
        valid_mask = ((positions >= offset) & (starts_count == earlier_count)).astype(jnp.float32)
        shifted = jnp.concatenate([jnp.zeros((offset, CHANNELS), jnp.float32), tokens_wide[:-offset]])
        pre_act = pre_act + conv_weight[offset][None, :] * shifted * valid_mask[:, None]
    activated = jax.nn.silu(pre_act).astype(jnp.bfloat16)

    blocks = total_tokens // TOKENS_PER_SHARD
    act_blocks = activated.reshape(blocks, TOKENS_PER_SHARD, SPACE_HEADS, HEAD_DIM)
    grad_blocks = out_grad.reshape(blocks, TOKENS_PER_SHARD, SPACE_HEADS, HEAD_DIM)
    b_blocks = b_proj.reshape(blocks, TOKENS_PER_SHARD, STATE)
    c_blocks = c_proj.reshape(blocks, TOKENS_PER_SHARD, STATE)
    log_blocks = log_decay.reshape(SPACE_HEADS, blocks, TOKENS_PER_SHARD).transpose(1, 0, 2)
    start_blocks = starts.reshape(blocks, TOKENS_PER_SHARD)

    def summarize(items):
        act_rows, grad_rows, b_block, c_block, log_block, start_block = items
        cum_decay, doc_count, weight_in, weight_out, carry_factor = block_setup(log_block, start_block)
        state_local, adjoint_local = block_states(act_rows, grad_rows, b_block, c_block, weight_in, weight_out)
        return carry_factor, state_local, adjoint_local

    carry_all, state_all, adjoint_all = lax.map(summarize, (act_blocks, grad_blocks, b_blocks, c_blocks, log_blocks, start_blocks))

    def forward_link(state, items):
        carry_factor, state_local = items
        return state_local + carry_factor[:, None, None] * state, state

    def backward_link(adjoint, items):
        carry_factor, adjoint_local = items
        return adjoint_local + carry_factor[:, None, None] * adjoint, adjoint

    empty = jnp.zeros((SPACE_HEADS, STATE, HEAD_DIM), jnp.float32)
    _, state_in_all = lax.scan(forward_link, empty, (carry_all, state_all))
    _, adjoint_in_all = lax.scan(backward_link, empty, (carry_all, adjoint_all), reverse=True)

    def block_grads(items):
        act_rows, grad_rows, b_block, c_block, log_block, start_block, state_local, state_in, adjoint_in = items
        cum_decay, doc_count, weight_in, weight_out, carry_factor = block_setup(log_block, start_block)
        scores = lax.dot_general(c_block, b_block, (((1,), (1,)), ((), ())), preferred_element_type=jnp.float32)
        score_grad, (heads_grad, cum_grad) = intra_heads(act_rows.transpose(1, 0, 2), grad_rows.transpose(1, 0, 2), cum_decay, doc_count, scores)
        act_extra, cum_extra, b_extra, c_extra = inter_terms(act_rows, grad_rows, b_block, c_block, weight_in, weight_out, carry_factor, state_local, state_in, adjoint_in)
        act_total = heads_grad.transpose(1, 0, 2) + act_extra + skip_gain[None, :, None] * grad_rows.astype(jnp.float32)
        b_grad = lax.dot_general(score_grad, c_block.astype(jnp.float32), (((0,), (0,)), ((), ())), precision=highest) + b_extra
        c_grad = jnp.dot(score_grad, b_block.astype(jnp.float32), precision=highest) + c_extra
        cum_total = cum_grad + cum_extra
        decay_grad = jnp.flip(jnp.cumsum(jnp.flip(cum_total, axis=1), axis=1), axis=1)
        return act_total, b_grad, c_grad, decay_grad

    act_grad, b_grad, c_grad, decay_grad = lax.map(block_grads, (act_blocks, grad_blocks, b_blocks, c_blocks, log_blocks, start_blocks, state_all, state_in_all, adjoint_in_all))
    pre_grad = act_grad.reshape(total_tokens, CHANNELS) * silu_slope(pre_act)
    in_grad = conv_weight[0][None, :] * pre_grad
    for offset in range(1, TAPS):
        later_count = jnp.concatenate([starts_count[offset:], jnp.full((offset,), -1, jnp.int32)])
        valid_mask = (later_count == starts_count).astype(jnp.float32)
        shifted = jnp.concatenate([pre_grad[offset:], jnp.zeros((offset, CHANNELS), jnp.float32)])
        in_grad = in_grad + conv_weight[offset][None, :] * shifted * valid_mask[:, None]
    return (in_grad,
            b_grad.reshape(total_tokens, STATE),
            c_grad.reshape(total_tokens, STATE),
            decay_grad.transpose(1, 0, 2).reshape(SPACE_HEADS, total_tokens))
```

```python
import functools

import jax
import jax.numpy as jnp
from jax import lax
from jax.experimental import pallas as pl
from jax.experimental.pallas import tpu as pltpu
from jax.sharding import PartitionSpec as P

MESH = pl.DeviceIdType.MESH
F32 = jnp.float32
BF16 = jnp.bfloat16
HIGHEST = lax.Precision.HIGHEST

ROWS = 256
HEADS = 8
WIDE = 512
STATE = 128
TAPS = 4
CUBE = 4

NN = (((1,), (0,)), ((), ()))
NT = (((1,), (1,)), ((), ()))
TN = (((0,), (0,)), ((), ()))


def dot(a, b, dims=NN):
    return lax.dot_general(a, b, dims, preferred_element_type=F32)


def exact_dot(a, b, dims=NN):
    return lax.dot_general(a, b, dims, precision=HIGHEST, preferred_element_type=F32)


def split(x):
    high = x.astype(BF16)
    return high, (x - high.astype(F32)).astype(BF16)


def wide_dot(x, y, dims=NN):
    high, low = split(x)
    return dot(high, y, dims) + dot(low, y, dims)


def scale_of(exponent):
    return jnp.exp2(exponent.astype(F32))


def exponent_of(largest):
    bits = jnp.floor(jnp.log(jnp.maximum(largest, 1e-36)) * 1.4426950408889634) + 1.0
    return jnp.clip(bits, -100.0, 100.0)


def code(x, exponent):
    return jnp.floor(x * scale_of(14.0 - exponent) + 0.5).astype(jnp.int32)


def pack(x):
    exponent = exponent_of(jnp.max(jnp.abs(x), axis=0, keepdims=True))
    return code(x, exponent).astype(jnp.int16), exponent


def pack_row(x):
    exponent = exponent_of(x)
    return code(x, exponent).astype(F32), exponent


def unpack(x, exponent):
    return x.astype(jnp.int32).astype(F32) * scale_of(exponent - 14.0)


def tile_of(*rows):
    row_of = lax.broadcasted_iota(jnp.int32, (16, 256), 0)
    tile = jnp.zeros((16, 256), F32)
    for i, row in enumerate(rows):
        tile = jnp.where(row_of == i, row, tile)
    return tile.astype(jnp.int32).astype(jnp.int16)


def kernel(
    chips,
    planes,
    tok_h,
    sta_h,
    log_h,
    bp_h,
    cp_h,
    gr_h,
    cw_h,
    cb_h,
    gain_h,
    in_h,
    sum_h,
    dec_h,
    o_in,
    o_sum,
    o_dec,
    tok,
    sta,
    log,
    bp,
    cp,
    gr,
    cw,
    cb,
    gain,
    ext,
    cnt,
    stk,
    act,
    slope,
    wact,
    wgr,
    win,
    wout,
    agr,
    sg,
    rowtot,
    xcol,
    loc,
    rx_full,
    rx_half,
    chip,
    l1,
    out2,
    l2,
    o3,
    full,
    rs_src,
    rs_dst,
    halo_s,
    halo_r,
    hb_s,
    hb_r,
    pg,
    pair_ss,
    pair_rs,
    halo_ss,
    halo_rs,
    l1_ss,
    l1_rs,
    l2_ss,
    l2_rs,
    l3_ss,
    l3_rs,
    fw_ss,
    fw_rs,
    sum_ss,
    sum_rs,
    ready,
    load,
    store,
):
    groups = chips // CUBE
    total = 2 * chips
    c = lax.axis_index("ctx")
    h = lax.axis_index("head")
    core = lax.rem(c, 2)
    other = 1 - core
    z = lax.div(c, 2)
    group = lax.div(z, CUBE)
    place = lax.rem(z, CUBE)
    after = (lax.rem(c + 1, total), h)
    before = (lax.rem(c + total - 1, total), h)
    partner = (2 * z + other, h)

    def in_cube(d):
        return lax.rem(place + d, CUBE)

    def cube_device(d):
        return (2 * (CUBE * group + in_cube(d)) + core, h)

    def other_group(d):
        return lax.rem(group + d, groups)

    def group_device(d):
        return (2 * (CUBE * other_group(d) + place) + core, h)

    def plane_head(d):
        return lax.rem(h + d, planes)

    barrier = pltpu.get_barrier_semaphore()
    peers = [after, before]
    peers += [cube_device(d) for d in range(1, CUBE)]
    nearby = sorted({1, groups - 1})
    peers += [group_device(d) for d in nearby]
    peers += [(c, plane_head(d)) for d in range(1, planes)]
    for peer in peers:
        pl.semaphore_signal(barrier, inc=1, device_id=peer, device_id_type=MESH)

    pairs = (
        (sta_h, sta),
        (log_h, log),
        (cp_h, cp),
        (gr_h, gr),
        (tok_h, tok),
        (cw_h, cw),
        (cb_h, cb),
        (bp_h, bp),
        (gain_h, gain),
    )
    loads = [
        pltpu.make_async_copy(src, dst, load.at[i]) for i, (src, dst) in enumerate(pairs)
    ]
    for copy in loads:
        copy.start()
    sends = []

    def send(src, dst, send_sem, recv_sem, device):
        copy = pltpu.make_async_remote_copy(
            src_ref=src,
            dst_ref=dst,
            send_sem=send_sem,
            recv_sem=recv_sem,
            device_id=device,
            device_id_type=MESH,
        )
        copy.start()
        sends.append(copy)
        return copy

    loads[0].wait()
    loads[1].wait()
    i0 = lax.broadcasted_iota(jnp.int32, (ROWS, ROWS), 0)
    i1 = lax.broadcasted_iota(jnp.int32, (ROWS, ROWS), 1)
    upper = (i0 <= i1).astype(F32)
    lower = (i0 >= i1).astype(F32)
    stk[0:HEADS] = log[...]
    stk[HEADS : 2 * HEADS] = jnp.broadcast_to(sta[...].astype(F32), (HEADS, ROWS))
    cum_row = exact_dot(stk[...], upper)
    cum_col = exact_dot(lower, stk[...], NT)
    cnt_row = cum_row[HEADS : HEADS + 1]
    cnt_col = cum_col[:, HEADS : HEADS + 1]
    cnt_last = cnt_col[ROWS - 1 : ROWS]
    log_col = cum_col[:, 0:HEADS]
    keep_in = (cnt_col == 0.0).astype(F32)
    keep_out = (cnt_col == cnt_last).astype(F32)
    cnt[0:8] = jnp.zeros((8, 128), F32)
    cnt[8 : 8 + ROWS] = jnp.broadcast_to(cnt_col, (ROWS, 128))
    cnt[8 + ROWS : 16 + ROWS] = jnp.broadcast_to(cnt_last, (8, 128))
    head_of = lax.broadcasted_iota(jnp.int32, (HEADS, WIDE), 0)
    lane_of = lax.broadcasted_iota(jnp.int32, (HEADS, WIDE), 1)
    pick = (lax.div(lane_of, WIDE // HEADS) == head_of).astype(F32)
    win[...] = exact_dot(jnp.exp(log_col) * keep_in, pick)
    wout[...] = exact_dot(jnp.exp(log_col[ROWS - 1 : ROWS] - log_col) * keep_out, pick)
    factor = win[ROWS - 1 : ROWS, :]
    for half in range(2):
        lanes = slice(256 * half, 256 * half + 256)
        for which in range(2):
            loc[which, half, STATE : STATE + 8] = jnp.broadcast_to(factor[:, lanes], (8, 256))

    loads[2].wait()
    loads[3].wait()
    for half in range(2):
        lanes = slice(256 * half, 256 * half + 256)
        high, low = split(win[:, lanes] * gr[:, lanes].astype(F32))
        wgr[0, :, lanes] = high
        wgr[1, :, lanes] = low
        loc[1, half, 0:STATE] = dot(cp[...], high, TN) + dot(cp[...], low, TN)

    for copy in loads[4:]:
        copy.wait()
    halo_s[...] = tok[ROWS - 16 :] * keep_out[ROWS - 16 :].astype(BF16)

    def convolve(first, rows):
        for chunk in range(4):
            lanes = slice(128 * chunk, 128 * chunk + 128)
            here = cnt[8 + first : 8 + first + rows]
            value = cb[:, lanes] + cw[0:1, lanes] * ext[8 + first : 8 + first + rows, lanes]
            for k in range(1, TAPS):
                rows_at = slice(8 - k + first, 8 - k + first + rows)
                valid = (here == cnt[rows_at]).astype(F32)
                value = value + cw[k : k + 1, lanes] * ext[rows_at, lanes] * valid
            sigma = 1.0 / (1.0 + jnp.exp(-value))
            act[first : first + rows, lanes] = (value * sigma).astype(BF16)
            slope[first : first + rows, lanes] = sigma * (1.0 + value * (1.0 - sigma))

    ext[0:8] = jnp.zeros((8, WIDE), F32)
    ext[8:] = tok[...].astype(F32)
    convolve(0, ROWS)

    def local_state(rows, half):
        lanes = slice(256 * half, 256 * half + 256)
        high, low = split(wout[rows, lanes] * act[rows, lanes].astype(F32))
        wact[0, rows, lanes] = high
        wact[1, rows, lanes] = low
        return dot(bp[rows], high, TN) + dot(bp[rows], low, TN)

    for half in range(2):
        loc[0, half, 0:STATE] = local_state(slice(16, ROWS), half)

    pl.semaphore_wait(barrier, len(peers))
    for d in nearby:
        pl.semaphore_signal(ready, inc=1, device_id=group_device(d), device_id_type=MESH)

    halo = send(halo_s, halo_r, halo_ss.at[0], halo_rs.at[0], after)
    halo.wait_recv()
    is_first = (c > 0).astype(F32)
    ext[0:8] = halo_r[8:16].astype(F32) * is_first
    convolve(0, 16)

    for half in range(2):
        loc[0, half, 0:STATE] += local_state(slice(0, 16), half)

    first = send(
        loc.at[core, other], rx_full.at[other], pair_ss.at[0], pair_rs.at[0], partner
    )
    second = send(loc.at[other, other], rx_half, pair_ss.at[1], pair_rs.at[1], partner)
    third = send(loc.at[core, core], rx_full.at[core], pair_ss.at[2], pair_rs.at[2], partner)
    first.wait_recv()
    second.wait_recv()
    f_own = loc[0, core, STATE : STATE + 1]
    f_other = rx_half[STATE : STATE + 1]
    is_late = core == 1
    factor_code, factor_exponent = pack_row(f_own * f_other)
    for s in range(CUBE):
        rows = slice(32 * s, 32 * s + 32)
        mine, e_mine = pack(rx_half[rows] + f_other * loc[core, core, rows])
        yours, e_yours = pack(loc[other, core, rows] + f_own * rx_full[core, rows])
        chip[s, pl.ds(pl.multiple_of(32 * core, 32), 32)] = mine
        chip[s, pl.ds(pl.multiple_of(32 * other, 32), 32)] = yours
        chip[s, 64:80] = tile_of(
            jnp.where(is_late, e_yours, e_mine),
            jnp.where(is_late, e_mine, e_yours),
            factor_exponent,
            factor_code,
        )

    l1[place] = chip[place]
    ups = []
    for d in range(1, CUBE):
        ups.append(
            send(chip.at[in_cube(d)], l1.at[place], l1_ss.at[d - 1], l1_rs.at[d - 1], cube_device(d))
        )

    gain_wide = exact_dot(jnp.broadcast_to(gain[...], (8, HEADS)), pick)[0:1]
    scores = dot(bp[...], cp[...], NT)
    bias = jnp.where((i0 <= i1) & (cnt_col == cnt_row), 0.0, -1e30)
    even = lax.broadcasted_iota(jnp.int32, (ROWS, 128), 1) < 64

    def intra(pair, begin):
        lanes = slice(128 * pair, 128 * pair + 128)
        parts = []
        for head in (2 * pair, 2 * pair + 1):
            decay = jnp.exp(cum_row[head : head + 1] - cum_col[:, head : head + 1] + bias)
            mixed = decay * scores
            parts.append(dot(mixed.astype(BF16), gr[:, lanes]))
            mine = even if head % 2 == 0 else ~even
            rows = jnp.where(mine, act[:, lanes].astype(F32), 0.0).astype(BF16)
            inner = dot(rows, gr[:, lanes], NT)
            if begin and head % 2 == 0:
                sg[...] = decay * inner
            else:
                sg[...] += decay * inner
            product = mixed * inner
            rowtot[head : head + 1] = jnp.sum(product, axis=0, keepdims=True)
            xcol[:, head : head + 1] = jnp.sum(product, axis=1, keepdims=True)
        agr[:, lanes] = jnp.where(even, parts[0], parts[1]) + gain_wide[:, lanes] * gr[
            :, lanes
        ].astype(F32)

    intra(0, True)
    intra(1, False)

    for copy in ups:
        copy.wait_recv()

    def unpack_slot(ref, j, arrays):
        tile = ref[j, 32 * arrays : 32 * arrays + 16].astype(jnp.int32).astype(F32)
        values = [
            unpack(ref[j, 32 * i : 32 * i + 32], tile[i : i + 1]) for i in range(arrays)
        ]
        factor = tile[arrays + 1 : arrays + 2] * scale_of(tile[arrays : arrays + 1] - 14.0)
        return values, factor

    slots = [unpack_slot(l1, j, 2) for j in range(CUBE)]

    def prefixes():
        values, factors = [jnp.zeros((32, 256), F32)], [jnp.ones((1, 256), F32)]
        for (state, _), f in slots:
            values.append(state + f * values[-1])
            factors.append(f * factors[-1])
        return values, factors

    def suffixes():
        values, factors = [jnp.zeros((32, 256), F32)], [jnp.ones((1, 256), F32)]
        for (_, adjoint), f in reversed(slots):
            values.append(adjoint + f * values[-1])
            factors.append(f * factors[-1])
        return values[::-1], factors[::-1]

    down, down_f = prefixes()
    up, up_f = suffixes()
    factor_code, factor_exponent = pack_row(down_f[CUBE])
    for kind, total_here in enumerate((down[CUBE], up[0])):
        coded, exponent = pack(total_here)
        out2[kind, 0:32] = coded
        out2[kind, 32:48] = tile_of(exponent, factor_exponent, factor_code)
    pl.semaphore_wait(ready, len(nearby))
    crosses = []
    for d in range(1, groups):
        kind = (other_group(d) < group).astype(jnp.int32)
        crosses.append(
            send(out2.at[kind], l2.at[group], l2_ss.at[d - 1], l2_rs.at[d - 1], group_device(d))
        )

    intra(2, False)
    intra(3, False)

    for copy in crosses:
        copy.wait_recv()
    totals = [unpack_slot(l2, u, 1) for u in range(groups)]
    from_before = jnp.zeros((32, 256), F32)
    for u in range(groups):
        (value,), f = totals[u]
        from_before = jnp.where(u < group, value + f * from_before, from_before)
    from_after = jnp.zeros((32, 256), F32)
    for u in reversed(range(groups)):
        (value,), f = totals[u]
        from_after = jnp.where(u > group, value + f * from_after, from_after)
    for j in range(CUBE):
        state, e_state = pack(down[j] + down_f[j] * from_before)
        adjoint, e_adjoint = pack(up[j + 1] + up_f[j + 1] * from_after)
        o3[j, 0:32] = state
        o3[j, 32:64] = adjoint
        o3[j, 64:80] = tile_of(e_state, e_adjoint)
    full[core, place] = o3[place]
    forwards = []
    backs = []
    for d in range(1, CUBE):
        backs.append(
            send(
                o3.at[in_cube(d)],
                full.at[core, place],
                l3_ss.at[d - 1],
                l3_rs.at[d - 1],
                cube_device(d),
            )
        )
    here = full.at[core, place]
    forwards.append(send(here, here, fw_ss.at[0], fw_rs.at[0], partner))

    high, low = split(sg[...])
    rs_src[:, 0:STATE] = dot(high, cp[...]) + dot(low, cp[...])
    rs_src[:, STATE:] = dot(high, bp[...], TN) + dot(low, bp[...], TN)

    for d in range(1, CUBE):
        backs[d - 1].wait_recv()
        slot = full.at[core, in_cube(CUBE - d)]
        forwards.append(send(slot, slot, fw_ss.at[d], fw_rs.at[d], partner))
    third.wait_recv()
    for copy in forwards:
        copy.wait_recv()

    late = (core == 1).astype(F32)
    early = 1.0 - late
    state_in, adjoint_in, end_row = [], [], []
    for half in range(2):
        f_other = rx_full[half, STATE : STATE + 1]
        received = rx_full[half, 0:STATE]
        f_own = loc[0, half, STATE : STATE + 1]
        tiles = full[half, :, 64:80].astype(jnp.int32).astype(F32)
        wide = unpack(full[half, :, 0:32], tiles[:, 0:1]).reshape(STATE, 256)
        state = late * received + (late * f_other + early) * wide
        wide = unpack(full[half, :, 32:64], tiles[:, 1:2]).reshape(STATE, 256)
        adjoint = early * received + (early * f_other + late) * wide
        state_out = loc[0, half, 0:STATE] + f_own * state
        end_row.append(jnp.sum(adjoint * state_out, axis=0, keepdims=True))
        state_in.append(state.astype(BF16))
        adjoint_in.append(adjoint.astype(BF16))

    b_part = rs_src[:, 0:STATE]
    c_part = rs_src[:, STATE:]
    for half in range(2):
        lanes = slice(256 * half, 256 * half + 256)
        for part in range(2):
            b_part = b_part + dot(wact[part, :, lanes], adjoint_in[half], NT)
            c_part = c_part + dot(wgr[part, :, lanes], state_in[half], NT)
    rs_src[:, 0:STATE] = b_part
    rs_src[:, STATE:] = c_part
    rs_dst[h] = rs_src[pl.ds(pl.multiple_of(16 * h, 16), 16)]
    sums = []
    for d in range(1, planes):
        rows = pl.ds(pl.multiple_of(16 * plane_head(d), 16), 16)
        sums.append(
            send(rs_src.at[rows], rs_dst.at[h], sum_ss.at[d - 1], sum_rs.at[d - 1], (c, plane_head(d)))
        )

    inter = jnp.zeros((HEADS, ROWS), F32)
    for half in range(2):
        lanes = slice(256 * half, 256 * half + 256)
        after_part = wout[:, lanes] * dot(bp[...], adjoint_in[half])
        before_part = win[:, lanes] * dot(cp[...], state_in[half])
        pg[0:ROWS, lanes] = (agr[:, lanes] + after_part) * slope[:, lanes]
        difference = before_part * gr[:, lanes].astype(F32) - after_part * act[:, lanes].astype(F32)
        inter = inter + exact_dot(pick[:, lanes], difference, NT)
    hb_s[...] = pg[0:8] * keep_in[0:8]
    back = send(hb_s, hb_r, halo_ss.at[1], halo_rs.at[1], before)

    ends = jnp.sum(pick * jnp.concatenate(end_row, axis=1), axis=1, keepdims=True)
    cum_total = rowtot[...] + inter - xcol[...].T[0:HEADS]
    o_dec[...] = exact_dot(cum_total, lower) + ends
    stores = [pltpu.make_async_copy(o_dec, dec_h, store.at[5])]
    stores[0].start()

    back.wait_recv()
    is_last = (c < total - 1).astype(F32)
    pg[ROWS:] = hb_r[...] * is_last
    for chunk in range(4):
        lanes = slice(128 * chunk, 128 * chunk + 128)
        value = cw[0:1, lanes] * pg[0:ROWS, lanes]
        for k in range(1, TAPS):
            valid = (cnt[8 + k : 8 + k + ROWS] == cnt[8 : 8 + ROWS]).astype(F32)
            value = value + cw[k : k + 1, lanes] * pg[k : k + ROWS, lanes] * valid
        o_in[:, lanes] = value
        stores.append(pltpu.make_async_copy(o_in.at[:, lanes], in_h.at[:, lanes], store.at[chunk]))
        stores[-1].start()

    for copy in sums:
        copy.wait_recv()
    result = rs_dst[0]
    for j in range(1, planes):
        result = result + rs_dst[j]
    o_sum[...] = result
    stores.append(pltpu.make_async_copy(o_sum, sum_h, store.at[4]))
    stores[-1].start()
    for copy in stores:
        copy.wait()

    for copy in sends:
        copy.wait_send()


def finish(a_in, a_sum, a_dec, o_in, o_b, o_c, o_dec, wide, sums, decay, load, store):
    def go(i, src, dst, sem):
        return pltpu.make_async_copy(src, dst, sem.at[i])

    quarter = ROWS // 4
    parts = [slice(quarter * i, quarter * i + quarter) for i in range(4)]
    pairs = [(a_in.at[p], wide.at[p], o_in.at[p]) for p in parts]
    loads = [go(i, src, mid, load) for i, (src, mid, _) in enumerate(pairs)]
    loads += [go(4, a_sum, sums, load), go(5, a_dec, decay, load)]
    stores = [go(i, mid, dst, store) for i, (_, mid, dst) in enumerate(pairs)]
    stores += [go(4, sums.at[:, 0:STATE], o_b, store), go(5, decay, o_dec, store)]
    stores += [go(6, sums.at[:, STATE : 2 * STATE], o_c, store)]
    for copy in loads:
        copy.start()
    for i in range(6):
        loads[i].wait()
        stores[i].start()
        if i == 4:
            stores[6].start()
    for copy in stores:
        copy.wait()


def body(tokens_in, starts, log_decay, b_proj, c_proj, out_grad, conv_weight, conv_bias, skip_gain):
    chips = lax.axis_size("ctx") // 2
    planes = lax.axis_size("head")
    groups = chips // CUBE
    own = ROWS // planes
    vmem = pltpu.VMEM
    dma = pltpu.SemaphoreType.DMA
    in_grad, sums, decay_grad = pl.pallas_call(
        functools.partial(kernel, chips, planes),
        out_shape=(
            jax.ShapeDtypeStruct((ROWS, WIDE), F32),
            jax.ShapeDtypeStruct((own, 2 * STATE), F32),
            jax.ShapeDtypeStruct((HEADS, ROWS), F32),
        ),
        in_specs=[pl.BlockSpec(memory_space=pltpu.HBM)] * 9,
        out_specs=[pl.BlockSpec(memory_space=pltpu.HBM)] * 3,
        scratch_shapes=[
            vmem((ROWS, WIDE), F32),
            vmem((own, 2 * STATE), F32),
            vmem((HEADS, ROWS), F32),
            vmem((ROWS, WIDE), BF16),
            vmem((1, ROWS), jnp.int32),
            vmem((HEADS, ROWS), F32),
            vmem((ROWS, STATE), BF16),
            vmem((ROWS, STATE), BF16),
            vmem((ROWS, WIDE), BF16),
            vmem((TAPS, WIDE), F32),
            vmem((1, WIDE), F32),
            vmem((1, HEADS), F32),
            vmem((8 + ROWS, WIDE), F32),
            vmem((16 + ROWS, 128), F32),
            vmem((2 * HEADS, ROWS), F32),
            vmem((ROWS, WIDE), BF16),
            vmem((ROWS, WIDE), F32),
            vmem((2, ROWS, WIDE), BF16),
            vmem((2, ROWS, WIDE), BF16),
            vmem((ROWS, WIDE), F32),
            vmem((ROWS, WIDE), F32),
            vmem((ROWS, WIDE), F32),
            vmem((ROWS, ROWS), F32),
            vmem((HEADS, ROWS), F32),
            vmem((ROWS, 128), F32),
            vmem((2, 2, STATE + 8, 256), F32),
            vmem((2, STATE + 8, 256), F32),
            vmem((STATE + 8, 256), F32),
            vmem((CUBE, 80, 256), jnp.int16),
            vmem((CUBE, 80, 256), jnp.int16),
            vmem((2, 48, 256), jnp.int16),
            vmem((groups, 48, 256), jnp.int16),
            vmem((CUBE, 80, 256), jnp.int16),
            vmem((2, CUBE, 80, 256), jnp.int16),
            vmem((ROWS, 2 * STATE), F32),
            vmem((planes, own, 2 * STATE), F32),
            vmem((16, WIDE), BF16),
            vmem((16, WIDE), BF16),
            vmem((8, WIDE), F32),
            vmem((8, WIDE), F32),
            vmem((8 + ROWS, WIDE), F32),
            dma((3,)),
            dma((3,)),
            dma((2,)),
            dma((2,)),
            dma((CUBE - 1,)),
            dma((CUBE - 1,)),
            dma((groups - 1,)),
            dma((groups - 1,)),
            dma((CUBE - 1,)),
            dma((CUBE - 1,)),
            dma((CUBE,)),
            dma((CUBE,)),
            dma((max(planes - 1, 1),)),
            dma((max(planes - 1, 1),)),
            pltpu.SemaphoreType.REGULAR,
            dma((9,)),
            dma((6,)),
        ],
        compiler_params=pltpu.CompilerParams(
            collective_id=0, has_side_effects=True, vmem_limit_bytes=63 * 1024 * 1024
        ),
        name="layer",
    )(
        tokens_in,
        starts.reshape(1, ROWS),
        log_decay,
        b_proj,
        c_proj,
        out_grad,
        conv_weight,
        conv_bias.reshape(1, WIDE),
        skip_gain.reshape(1, HEADS),
    )
    in_grad, b_grad, c_grad, decay_grad = pl.pallas_call(
        finish,
        out_shape=(
            jax.ShapeDtypeStruct((ROWS, WIDE), F32),
            jax.ShapeDtypeStruct((own, STATE), F32),
            jax.ShapeDtypeStruct((own, STATE), F32),
            jax.ShapeDtypeStruct((HEADS, ROWS), F32),
        ),
        in_specs=[pl.BlockSpec(memory_space=pl.ANY)] * 3,
        out_specs=[pl.BlockSpec(memory_space=pltpu.HBM)] * 4,
        scratch_shapes=[
            vmem((ROWS, WIDE), F32),
            vmem((own, 2 * STATE), F32),
            vmem((HEADS, ROWS), F32),
            dma((6,)),
            dma((7,)),
        ],
        compiler_params=pltpu.CompilerParams(vmem_limit_bytes=63 * 1024 * 1024),
        name="finish",
    )(in_grad, sums, decay_grad)
    return (in_grad, b_grad, c_grad, decay_grad)


def solution(mesh):
    placed = (
        P("ctx", "head"),
        P("ctx"),
        P("head", "ctx"),
        P("ctx", None),
        P("ctx", None),
        P("ctx", "head"),
        P(None, "head"),
        P("head"),
        P("head"),
    )
    return jax.shard_map(
        body,
        mesh=mesh,
        in_specs=placed,
        out_specs=(
            P("ctx", "head"),
            P(("ctx", "head"), None),
            P(("ctx", "head"), None),
            P("head", "ctx"),
        ),
        check_vma=False,
    )
```

```python
import functools

import jax
import jax.numpy as jnp
from jax import lax
from jax.experimental import pallas as pl
from jax.experimental.pallas import tpu as pltpu
from jax.sharding import PartitionSpec as P

MESH = pl.DeviceIdType.MESH
F32 = jnp.float32
BF16 = jnp.bfloat16
HIGHEST = lax.Precision.HIGHEST

ROWS = 256
HEADS = 8
WIDE = 512
STATE = 128
TAPS = 4
CUBE = 4

NN = (((1,), (0,)), ((), ()))
NT = (((1,), (1,)), ((), ()))
TN = (((0,), (0,)), ((), ()))


def dot(a, b, dims=NN):
    return lax.dot_general(a, b, dims, preferred_element_type=F32)


def exact_dot(a, b, dims=NN):
    return lax.dot_general(a, b, dims, precision=HIGHEST, preferred_element_type=F32)


def split(x):
    high = x.astype(BF16)
    return high, (x - high.astype(F32)).astype(BF16)


def wide_dot(x, y, dims=NN):
    high, low = split(x)
    return dot(high, y, dims) + dot(low, y, dims)


def scale_of(exponent):
    return jnp.exp2(exponent.astype(F32))


def exponent_of(largest):
    bits = jnp.floor(jnp.log(jnp.maximum(largest, 1e-36)) * 1.4426950408889634) + 1.0
    return jnp.clip(bits, -100.0, 100.0)


def code(x, exponent):
    return jnp.floor(x * scale_of(14.0 - exponent) + 0.5).astype(jnp.int32)


def pack(x):
    exponent = exponent_of(jnp.max(jnp.abs(x), axis=0, keepdims=True))
    return code(x, exponent).astype(jnp.int16), exponent


def pack_row(x):
    exponent = exponent_of(x)
    return code(x, exponent).astype(F32), exponent


def unpack(x, exponent):
    return x.astype(jnp.int32).astype(F32) * scale_of(exponent - 14.0)


def tile_of(*rows):
    row_of = lax.broadcasted_iota(jnp.int32, (16, 128), 0)
    tile = jnp.zeros((16, 128), F32)
    for i, row in enumerate(rows):
        tile = jnp.where(row_of == i, row, tile)
    return tile.astype(jnp.int32).astype(jnp.int16)


def block_of(place):
    row, lane = 64 * (place // 2), 128 * (place % 2)
    return slice(row, row + 64), slice(lane, lane + 128)


def kernel(
    chips,
    planes,
    tok_h,
    sta_h,
    log_h,
    bp_h,
    cp_h,
    gr_h,
    cw_h,
    cb_h,
    gain_h,
    in_h,
    sum_h,
    dec_h,
    o_in,
    o_dec,
    tok,
    sta,
    log,
    bp,
    cp,
    gr,
    cw,
    cb,
    gain,
    ext,
    cnt,
    stk,
    act,
    slope,
    wact,
    wgr,
    win,
    wout,
    agr,
    sg,
    rowtot,
    xcol,
    loc,
    rx_full,
    rx_half,
    chip,
    l1,
    out2,
    l2,
    o3,
    full,
    rs_src,
    rs_out,
    halo_s,
    halo_r,
    hb_s,
    hb_r,
    pg,
    pair_ss,
    pair_rs,
    halo_ss,
    halo_rs,
    l1_ss,
    l1_rs,
    l2_ss,
    l2_rs,
    l3_ss,
    l3_rs,
    fw_ss,
    fw_rs,
    sum_ss,
    sum_rs,
    ready,
    load,
    store,
):
    groups = chips // CUBE
    total = 2 * chips
    c = lax.axis_index("ctx")
    h = lax.axis_index("head")
    core = lax.rem(c, 2)
    other = 1 - core
    z = lax.div(c, 2)
    group = lax.div(z, CUBE)
    place = lax.rem(z, CUBE)
    after = (lax.rem(c + 1, total), h)
    before = (lax.rem(c + total - 1, total), h)
    partner = (2 * z + other, h)

    def in_cube(d):
        return lax.rem(place + d, CUBE)

    def cube_device(d):
        return (2 * (CUBE * group + in_cube(d)) + core, h)

    def other_group(d):
        return lax.rem(group + d, groups)

    def group_device(d):
        return (2 * (CUBE * other_group(d) + place) + core, h)

    def plane_head(d):
        return lax.rem(h + d, planes)

    barrier = pltpu.get_barrier_semaphore()
    peers = [after, before]
    peers += [cube_device(d) for d in range(1, CUBE)]
    nearby = sorted({1, groups - 1})
    peers += [group_device(d) for d in nearby]
    peers += [(c, plane_head(d)) for d in range(1, planes)]
    for peer in peers:
        pl.semaphore_signal(barrier, inc=1, device_id=peer, device_id_type=MESH)

    pairs = (
        (sta_h, sta),
        (log_h, log),
        (cp_h, cp),
        (gr_h, gr),
        (tok_h, tok),
        (cw_h, cw),
        (cb_h, cb),
        (bp_h, bp),
        (gain_h, gain),
    )
    loads = [
        pltpu.make_async_copy(src, dst, load.at[i]) for i, (src, dst) in enumerate(pairs)
    ]
    for copy in loads:
        copy.start()
    sends = []

    def send(src, dst, send_sem, recv_sem, device):
        copy = pltpu.make_async_remote_copy(
            src_ref=src,
            dst_ref=dst,
            send_sem=send_sem,
            recv_sem=recv_sem,
            device_id=device,
            device_id_type=MESH,
        )
        copy.start()
        sends.append(copy)
        return copy

    loads[0].wait()
    loads[1].wait()
    i0 = lax.broadcasted_iota(jnp.int32, (ROWS, ROWS), 0)
    i1 = lax.broadcasted_iota(jnp.int32, (ROWS, ROWS), 1)
    upper = (i0 <= i1).astype(F32)
    lower = (i0 >= i1).astype(F32)
    stk[0:HEADS] = log[...]
    stk[HEADS : 2 * HEADS] = jnp.broadcast_to(sta[...].astype(F32), (HEADS, ROWS))
    cum_row = exact_dot(stk[...], upper)
    cum_col = exact_dot(lower, stk[...], NT)
    cnt_row = cum_row[HEADS : HEADS + 1]
    cnt_col = cum_col[:, HEADS : HEADS + 1]
    cnt_last = cnt_col[ROWS - 1 : ROWS]
    log_col = cum_col[:, 0:HEADS]
    keep_in = (cnt_col == 0.0).astype(F32)
    keep_out = (cnt_col == cnt_last).astype(F32)
    cnt[0:8] = jnp.zeros((8, 128), F32)
    cnt[8 : 8 + ROWS] = jnp.broadcast_to(cnt_col, (ROWS, 128))
    cnt[8 + ROWS : 16 + ROWS] = jnp.broadcast_to(cnt_last, (8, 128))
    head_of = lax.broadcasted_iota(jnp.int32, (HEADS, WIDE), 0)
    lane_of = lax.broadcasted_iota(jnp.int32, (HEADS, WIDE), 1)
    pick = (lax.div(lane_of, WIDE // HEADS) == head_of).astype(F32)
    win[...] = exact_dot(jnp.exp(log_col) * keep_in, pick)
    wout[...] = exact_dot(jnp.exp(log_col[ROWS - 1 : ROWS] - log_col) * keep_out, pick)
    factor = win[ROWS - 1 : ROWS, :]
    for half in range(2):
        lanes = slice(256 * half, 256 * half + 256)
        for which in range(2):
            loc[which, half, STATE : STATE + 8] = jnp.broadcast_to(factor[:, lanes], (8, 256))

    loads[2].wait()
    loads[3].wait()
    for half in range(2):
        lanes = slice(256 * half, 256 * half + 256)
        high, low = split(win[:, lanes] * gr[:, lanes].astype(F32))
        wgr[0, :, lanes] = high
        wgr[1, :, lanes] = low
        loc[1, half, 0:STATE] = dot(cp[...], high, TN) + dot(cp[...], low, TN)

    for copy in loads[4:]:
        copy.wait()
    halo_s[...] = tok[ROWS - 16 :] * keep_out[ROWS - 16 :].astype(BF16)

    def convolve(first, rows):
        for chunk in range(4):
            lanes = slice(128 * chunk, 128 * chunk + 128)
            here = cnt[8 + first : 8 + first + rows]
            value = cb[:, lanes] + cw[0:1, lanes] * ext[8 + first : 8 + first + rows, lanes]
            for k in range(1, TAPS):
                rows_at = slice(8 - k + first, 8 - k + first + rows)
                valid = (here == cnt[rows_at]).astype(F32)
                value = value + cw[k : k + 1, lanes] * ext[rows_at, lanes] * valid
            sigma = 1.0 / (1.0 + jnp.exp(-value))
            act[first : first + rows, lanes] = (value * sigma).astype(BF16)
            slope[first : first + rows, lanes] = sigma * (1.0 + value * (1.0 - sigma))

    ext[0:8] = jnp.zeros((8, WIDE), F32)
    ext[8:] = tok[...].astype(F32)
    convolve(0, ROWS)

    def local_state(rows, half):
        lanes = slice(256 * half, 256 * half + 256)
        high, low = split(wout[rows, lanes] * act[rows, lanes].astype(F32))
        wact[0, rows, lanes] = high
        wact[1, rows, lanes] = low
        return dot(bp[rows], high, TN) + dot(bp[rows], low, TN)

    for half in range(2):
        loc[0, half, 0:STATE] = local_state(slice(16, ROWS), half)

    pl.semaphore_wait(barrier, len(peers))
    for d in nearby:
        pl.semaphore_signal(ready, inc=1, device_id=group_device(d), device_id_type=MESH)

    halo = send(halo_s, halo_r, halo_ss.at[0], halo_rs.at[0], after)
    halo.wait_recv()
    is_first = (c > 0).astype(F32)
    ext[0:8] = halo_r[8:16].astype(F32) * is_first
    convolve(0, 16)

    for half in range(2):
        loc[0, half, 0:STATE] += local_state(slice(0, 16), half)

    first = send(
        loc.at[core, other], rx_full.at[other], pair_ss.at[0], pair_rs.at[0], partner
    )
    second = send(loc.at[other, other], rx_half, pair_ss.at[1], pair_rs.at[1], partner)
    third = send(loc.at[core, core], rx_full.at[core], pair_ss.at[2], pair_rs.at[2], partner)
    first.wait_recv()
    second.wait_recv()
    f_own = loc[0, core, STATE : STATE + 1]
    f_other = rx_half[STATE : STATE + 1]
    is_late = core == 1
    factor_code, factor_exponent = pack_row(f_own * f_other)
    for s in range(CUBE):
        rows, lanes = block_of(s)
        mine, e_mine = pack(rx_half[rows, lanes] + f_other[:, lanes] * loc[core, core, rows, lanes])
        yours, e_yours = pack(
            loc[other, core, rows, lanes] + f_own[:, lanes] * rx_full[core, rows, lanes]
        )
        chip[s, pl.ds(pl.multiple_of(64 * core, 64), 64)] = mine
        chip[s, pl.ds(pl.multiple_of(64 * other, 64), 64)] = yours
        chip[s, 128:144] = tile_of(
            jnp.where(is_late, e_yours, e_mine),
            jnp.where(is_late, e_mine, e_yours),
            factor_exponent[:, lanes],
            factor_code[:, lanes],
        )

    l1[place] = chip[place]
    ups = []
    for d in range(1, CUBE):
        ups.append(
            send(chip.at[in_cube(d)], l1.at[place], l1_ss.at[d - 1], l1_rs.at[d - 1], cube_device(d))
        )

    gain_wide = exact_dot(jnp.broadcast_to(gain[...], (8, HEADS)), pick)[0:1]
    scores = dot(bp[...], cp[...], NT)
    bias = jnp.where((i0 <= i1) & (cnt_col == cnt_row), 0.0, -1e30)
    even = lax.broadcasted_iota(jnp.int32, (ROWS, 128), 1) < 64

    def intra(pair, begin):
        lanes = slice(128 * pair, 128 * pair + 128)
        parts = []
        for head in (2 * pair, 2 * pair + 1):
            decay = jnp.exp(cum_row[head : head + 1] - cum_col[:, head : head + 1] + bias)
            mixed = decay * scores
            parts.append(dot(mixed.astype(BF16), gr[:, lanes]))
            mine = even if head % 2 == 0 else ~even
            rows = jnp.where(mine, act[:, lanes].astype(F32), 0.0).astype(BF16)
            inner = dot(rows, gr[:, lanes], NT)
            if begin and head % 2 == 0:
                sg[...] = decay * inner
            else:
                sg[...] += decay * inner
            product = mixed * inner
            rowtot[head : head + 1] = jnp.sum(product, axis=0, keepdims=True)
            xcol[:, head : head + 1] = jnp.sum(product, axis=1, keepdims=True)
        agr[:, lanes] = jnp.where(even, parts[0], parts[1]) + gain_wide[:, lanes] * gr[
            :, lanes
        ].astype(F32)

    intra(0, True)
    intra(1, False)

    for copy in ups:
        copy.wait_recv()

    def unpack_slot(ref, j, arrays):
        tile = ref[j, 64 * arrays : 64 * arrays + 16].astype(jnp.int32).astype(F32)
        values = [
            unpack(ref[j, 64 * i : 64 * i + 64], tile[i : i + 1]) for i in range(arrays)
        ]
        factor = tile[arrays + 1 : arrays + 2] * scale_of(tile[arrays : arrays + 1] - 14.0)
        return values, factor

    slots = [unpack_slot(l1, j, 2) for j in range(CUBE)]

    def prefixes():
        values, factors = [jnp.zeros((64, 128), F32)], [jnp.ones((1, 128), F32)]
        for (state, _), f in slots:
            values.append(state + f * values[-1])
            factors.append(f * factors[-1])
        return values, factors

    def suffixes():
        values, factors = [jnp.zeros((64, 128), F32)], [jnp.ones((1, 128), F32)]
        for (_, adjoint), f in reversed(slots):
            values.append(adjoint + f * values[-1])
            factors.append(f * factors[-1])
        return values[::-1], factors[::-1]

    down, down_f = prefixes()
    up, up_f = suffixes()
    factor_code, factor_exponent = pack_row(down_f[CUBE])
    for kind, total_here in enumerate((down[CUBE], up[0])):
        coded, exponent = pack(total_here)
        out2[kind, 0:64] = coded
        out2[kind, 64:80] = tile_of(exponent, factor_exponent, factor_code)
    pl.semaphore_wait(ready, len(nearby))
    crosses = []
    for d in range(1, groups):
        kind = (other_group(d) < group).astype(jnp.int32)
        crosses.append(
            send(out2.at[kind], l2.at[group], l2_ss.at[d - 1], l2_rs.at[d - 1], group_device(d))
        )

    intra(2, False)
    intra(3, False)

    for copy in crosses:
        copy.wait_recv()
    totals = [unpack_slot(l2, u, 1) for u in range(groups)]
    from_before = jnp.zeros((64, 128), F32)
    for u in range(groups):
        (value,), f = totals[u]
        from_before = jnp.where(u < group, value + f * from_before, from_before)
    from_after = jnp.zeros((64, 128), F32)
    for u in reversed(range(groups)):
        (value,), f = totals[u]
        from_after = jnp.where(u > group, value + f * from_after, from_after)
    for j in range(CUBE):
        state, e_state = pack(down[j] + down_f[j] * from_before)
        adjoint, e_adjoint = pack(up[j + 1] + up_f[j + 1] * from_after)
        o3[j, 0:64] = state
        o3[j, 64:128] = adjoint
        o3[j, 128:144] = tile_of(e_state, e_adjoint)
    full[core, place] = o3[place]
    forwards = []
    backs = []
    for d in range(1, CUBE):
        backs.append(
            send(
                o3.at[in_cube(d)],
                full.at[core, place],
                l3_ss.at[d - 1],
                l3_rs.at[d - 1],
                cube_device(d),
            )
        )
    here = full.at[core, place]
    forwards.append(send(here, here, fw_ss.at[0], fw_rs.at[0], partner))

    high, low = split(sg[...])
    rs_src[:, 0:STATE] = dot(high, cp[...]) + dot(low, cp[...])
    rs_src[:, STATE:] = dot(high, bp[...], TN) + dot(low, bp[...], TN)

    for d in range(1, CUBE):
        backs[d - 1].wait_recv()
        slot = full.at[core, in_cube(CUBE - d)]
        forwards.append(send(slot, slot, fw_ss.at[d], fw_rs.at[d], partner))
    third.wait_recv()
    for copy in forwards:
        copy.wait_recv()

    def incoming(half, which):
        blocks = []
        for s in range(CUBE):
            tile = full[half, s, 128:144].astype(jnp.int32).astype(F32)
            blocks.append(
                unpack(full[half, s, 64 * which : 64 * which + 64], tile[which : which + 1])
            )
        top = jnp.concatenate(blocks[0:2], axis=1)
        return jnp.concatenate([top, jnp.concatenate(blocks[2:4], axis=1)], axis=0)

    late = (core == 1).astype(F32)
    early = 1.0 - late
    state_in, adjoint_in, end_row = [], [], []
    for half in range(2):
        f_other = rx_full[half, STATE : STATE + 1]
        received = rx_full[half, 0:STATE]
        f_own = loc[0, half, STATE : STATE + 1]
        wide = incoming(half, 0)
        state = late * received + (late * f_other + early) * wide
        wide = incoming(half, 1)
        adjoint = early * received + (early * f_other + late) * wide
        state_out = loc[0, half, 0:STATE] + f_own * state
        end_row.append(jnp.sum(adjoint * state_out, axis=0, keepdims=True))
        state_in.append(split(state))
        adjoint_in.append(split(adjoint))

    b_part = rs_src[:, 0:STATE]
    c_part = rs_src[:, STATE:]
    for half in range(2):
        lanes = slice(256 * half, 256 * half + 256)
        for left, right in ((0, 0), (1, 0), (0, 1)):
            b_part = b_part + dot(wact[left, :, lanes], adjoint_in[half][right], NT)
            c_part = c_part + dot(wgr[left, :, lanes], state_in[half][right], NT)
    rs_out[:, 0:STATE] = b_part.astype(BF16)
    rs_out[:, STATE:] = c_part.astype(BF16)
    keep = pltpu.make_async_copy(
        rs_out.at[pl.ds(pl.multiple_of(16 * h, 16), 16)], sum_h.at[h], store.at[4]
    )
    keep.start()
    sums = []
    for d in range(1, planes):
        rows = pl.ds(pl.multiple_of(16 * plane_head(d), 16), 16)
        sums.append(
            send(rs_out.at[rows], sum_h.at[h], sum_ss.at[d - 1], sum_rs.at[d - 1], (c, plane_head(d)))
        )

    inter = jnp.zeros((HEADS, ROWS), F32)
    for half in range(2):
        lanes = slice(256 * half, 256 * half + 256)
        after_part = wout[:, lanes] * dot(bp[...], adjoint_in[half][0])
        before_part = win[:, lanes] * dot(cp[...], state_in[half][0])
        pg[0:ROWS, lanes] = (agr[:, lanes] + after_part) * slope[:, lanes]
        difference = before_part * gr[:, lanes].astype(F32) - after_part * act[:, lanes].astype(F32)
        inter = inter + exact_dot(pick[:, lanes], difference, NT)
    hb_s[...] = pg[0:8] * keep_in[0:8]
    back = send(hb_s, hb_r, halo_ss.at[1], halo_rs.at[1], before)

    ends = jnp.sum(pick * jnp.concatenate(end_row, axis=1), axis=1, keepdims=True)
    cum_total = rowtot[...] + inter - xcol[...].T[0:HEADS]
    o_dec[...] = exact_dot(cum_total, lower) + ends
    stores = [pltpu.make_async_copy(o_dec, dec_h, store.at[5])]
    stores[0].start()

    back.wait_recv()
    is_last = (c < total - 1).astype(F32)
    pg[ROWS:] = hb_r[...] * is_last
    for chunk in range(4):
        lanes = slice(128 * chunk, 128 * chunk + 128)
        value = cw[0:1, lanes] * pg[0:ROWS, lanes]
        for k in range(1, TAPS):
            valid = (cnt[8 + k : 8 + k + ROWS] == cnt[8 : 8 + ROWS]).astype(F32)
            value = value + cw[k : k + 1, lanes] * pg[k : k + ROWS, lanes] * valid
        o_in[:, lanes] = value
        stores.append(pltpu.make_async_copy(o_in.at[:, lanes], in_h.at[:, lanes], store.at[chunk]))
        stores[-1].start()

    for copy in sums:
        copy.wait_recv()
    stores.append(keep)
    for copy in stores:
        copy.wait()

    for copy in sends:
        copy.wait_send()


def finish(a_in, a_sum, a_dec, o_in, o_b, o_c, o_dec, wide, sums, both, decay, load, store):
    def go(i, src, dst, sem):
        return pltpu.make_async_copy(src, dst, sem.at[i])

    half = ROWS // 2
    triples = [(a_sum, sums, None)]
    triples += [(a_in.at[p], wide.at[p], o_in.at[p]) for p in (pl.ds(0, half), pl.ds(half, half))]
    triples += [(a_dec, decay, o_dec)]
    loads = [go(i, src, mid, load) for i, (src, mid, _) in enumerate(triples)]
    stores = [go(0, both.at[0], o_b, store)]
    stores += [go(i, mid, dst, store) for i, (_, mid, dst) in enumerate(triples) if i > 0]
    stores += [go(4, both.at[1], o_c, store)]
    for copy in loads:
        copy.start()
    for i in range(1, 4):
        loads[i].wait()
        stores[i].start()
    loads[0].wait()
    total = sums[0].astype(F32)
    for j in range(1, sums.shape[0]):
        total = total + sums[j].astype(F32)
    both[0] = total[:, 0:STATE]
    both[1] = total[:, STATE:]
    stores[0].start()
    stores[4].start()
    for copy in stores:
        copy.wait()


def body(tokens_in, starts, log_decay, b_proj, c_proj, out_grad, conv_weight, conv_bias, skip_gain):
    chips = lax.axis_size("ctx") // 2
    planes = lax.axis_size("head")
    groups = chips // CUBE
    own = ROWS // planes
    vmem = pltpu.VMEM
    dma = pltpu.SemaphoreType.DMA
    in_grad, sums, decay_grad = pl.pallas_call(
        functools.partial(kernel, chips, planes),
        out_shape=(
            jax.ShapeDtypeStruct((ROWS, WIDE), F32),
            jax.ShapeDtypeStruct((planes, own, 2 * STATE), BF16),
            jax.ShapeDtypeStruct((HEADS, ROWS), F32),
        ),
        in_specs=[pl.BlockSpec(memory_space=pltpu.HBM)] * 9,
        out_specs=[pl.BlockSpec(memory_space=pltpu.HBM)] * 3,
        scratch_shapes=[
            vmem((ROWS, WIDE), F32),
            vmem((HEADS, ROWS), F32),
            vmem((ROWS, WIDE), BF16),
            vmem((1, ROWS), jnp.int32),
            vmem((HEADS, ROWS), F32),
            vmem((ROWS, STATE), BF16),
            vmem((ROWS, STATE), BF16),
            vmem((ROWS, WIDE), BF16),
            vmem((TAPS, WIDE), F32),
            vmem((1, WIDE), F32),
            vmem((1, HEADS), F32),
            vmem((8 + ROWS, WIDE), F32),
            vmem((16 + ROWS, 128), F32),
            vmem((2 * HEADS, ROWS), F32),
            vmem((ROWS, WIDE), BF16),
            vmem((ROWS, WIDE), F32),
            vmem((2, ROWS, WIDE), BF16),
            vmem((2, ROWS, WIDE), BF16),
            vmem((ROWS, WIDE), F32),
            vmem((ROWS, WIDE), F32),
            vmem((ROWS, WIDE), F32),
            vmem((ROWS, ROWS), F32),
            vmem((HEADS, ROWS), F32),
            vmem((ROWS, 128), F32),
            vmem((2, 2, STATE + 8, 256), F32),
            vmem((2, STATE + 8, 256), F32),
            vmem((STATE + 8, 256), F32),
            vmem((CUBE, 144, 128), jnp.int16),
            vmem((CUBE, 144, 128), jnp.int16),
            vmem((2, 80, 128), jnp.int16),
            vmem((groups, 80, 128), jnp.int16),
            vmem((CUBE, 144, 128), jnp.int16),
            vmem((2, CUBE, 144, 128), jnp.int16),
            vmem((ROWS, 2 * STATE), F32),
            vmem((ROWS, 2 * STATE), BF16),
            vmem((16, WIDE), BF16),
            vmem((16, WIDE), BF16),
            vmem((8, WIDE), F32),
            vmem((8, WIDE), F32),
            vmem((8 + ROWS, WIDE), F32),
            dma((3,)),
            dma((3,)),
            dma((2,)),
            dma((2,)),
            dma((CUBE - 1,)),
            dma((CUBE - 1,)),
            dma((groups - 1,)),
            dma((groups - 1,)),
            dma((CUBE - 1,)),
            dma((CUBE - 1,)),
            dma((CUBE,)),
            dma((CUBE,)),
            dma((max(planes - 1, 1),)),
            dma((max(planes - 1, 1),)),
            pltpu.SemaphoreType.REGULAR,
            dma((9,)),
            dma((6,)),
        ],
        compiler_params=pltpu.CompilerParams(
            collective_id=0, has_side_effects=True, vmem_limit_bytes=63 * 1024 * 1024
        ),
        name="layer",
    )(
        tokens_in,
        starts.reshape(1, ROWS),
        log_decay,
        b_proj,
        c_proj,
        out_grad,
        conv_weight,
        conv_bias.reshape(1, WIDE),
        skip_gain.reshape(1, HEADS),
    )
    in_grad, b_grad, c_grad, decay_grad = pl.pallas_call(
        finish,
        out_shape=(
            jax.ShapeDtypeStruct((ROWS, WIDE), F32),
            jax.ShapeDtypeStruct((own, STATE), F32),
            jax.ShapeDtypeStruct((own, STATE), F32),
            jax.ShapeDtypeStruct((HEADS, ROWS), F32),
        ),
        in_specs=[pl.BlockSpec(memory_space=pl.ANY)] * 3,
        out_specs=[pl.BlockSpec(memory_space=pltpu.HBM)] * 4,
        scratch_shapes=[
            vmem((ROWS, WIDE), F32),
            vmem((planes, own, 2 * STATE), BF16),
            vmem((2, own, STATE), F32),
            vmem((HEADS, ROWS), F32),
            dma((4,)),
            dma((5,)),
        ],
        compiler_params=pltpu.CompilerParams(vmem_limit_bytes=63 * 1024 * 1024),
        name="finish",
    )(in_grad, sums, decay_grad)
    return (in_grad, b_grad, c_grad, decay_grad)


def solution(mesh):
    placed = (
        P("ctx", "head"),
        P("ctx"),
        P("head", "ctx"),
        P("ctx", None),
        P("ctx", None),
        P("ctx", "head"),
        P(None, "head"),
        P("head"),
        P("head"),
    )
    return jax.shard_map(
        body,
        mesh=mesh,
        in_specs=placed,
        out_specs=(
            P("ctx", "head"),
            P(("ctx", "head"), None),
            P(("ctx", "head"), None),
            P("head", "ctx"),
        ),
        check_vma=False,
    )
```

```python
import functools
import math

import jax
import jax.numpy as jnp
from jax import lax
from jax.experimental import pallas as pl
from jax.experimental.pallas import tpu as pltpu
from jax.sharding import PartitionSpec as P

MESH = pl.DeviceIdType.MESH
F32 = jnp.float32
BF16 = jnp.bfloat16
HIGHEST = lax.Precision.HIGHEST

ROWS = 256
HEADS = 8
WIDE = 512
STATE = 128
TAPS = 4
CUBE = 4

NN = (((1,), (0,)), ((), ()))
NT = (((1,), (1,)), ((), ()))
TN = (((0,), (0,)), ((), ()))


def dot(a, b, dims=NN):
    return lax.dot_general(a, b, dims, preferred_element_type=F32)


def exact_dot(a, b, dims=NN):
    return lax.dot_general(a, b, dims, precision=HIGHEST, preferred_element_type=F32)


def split(x):
    high = x.astype(BF16)
    return high, (x - high.astype(F32)).astype(BF16)


def sum_dot(x, ones, dims=NN, first=True):
    high = x.astype(BF16)
    rest = x - high.astype(F32)
    middle = rest.astype(BF16)
    low = (rest - middle.astype(F32)).astype(BF16)
    parts = [dot(p, ones, dims) if first else dot(ones, p, dims) for p in (high, middle, low)]
    return parts[0] + (parts[1] + parts[2])


def wide_dot(x, y, dims=NN):
    high, low = split(x)
    return dot(high, y, dims) + dot(low, y, dims)


def scale_of(exponent):
    return jnp.exp2(exponent.astype(F32))


def exponent_of(largest):
    bits = jnp.floor(jnp.log(jnp.maximum(largest, 1e-36)) * 1.4426950408889634) + 1.0
    return jnp.clip(bits, -100.0, 100.0)


def code(x, exponent):
    return jnp.floor(x * scale_of(14.0 - exponent) + 0.5).astype(jnp.int32)


def pack(x):
    exponent = exponent_of(jnp.max(jnp.abs(x), axis=0, keepdims=True))
    return code(x, exponent).astype(jnp.int16), exponent


def pack_row(x):
    exponent = exponent_of(x)
    return code(x, exponent).astype(F32), exponent


def unpack(x, exponent):
    return x.astype(jnp.int32).astype(F32) * scale_of(exponent - 14.0)


def tile_of(*rows):
    row_of = lax.broadcasted_iota(jnp.int32, (16, 128), 0)
    tile = jnp.zeros((16, 128), F32)
    for i, row in enumerate(rows):
        tile = jnp.where(row_of == i, row, tile)
    return tile.astype(jnp.int32).astype(jnp.int16)


def block_of(place):
    row, lane = 64 * (place // 2), 128 * (place % 2)
    return slice(row, row + 64), slice(lane, lane + 128)


def kernel(
    chips,
    planes,
    tok_h,
    sta_h,
    log_h,
    bp_h,
    cp_h,
    gr_h,
    cw_h,
    cb_h,
    gain_h,
    in_h,
    sum_h,
    dec_h,
    o_in,
    o_dec,
    tok,
    sta,
    log,
    bp,
    cp,
    gr,
    cw,
    cb,
    gain,
    ext,
    cnt,
    stk,
    act,
    slope,
    wact,
    wgr,
    win,
    wout,
    agr,
    sg,
    rowtot,
    xcol,
    loc,
    rx_full,
    rx_half,
    chip,
    l1,
    out2,
    l2,
    o3,
    full,
    rs_src,
    rs_out,
    halo_s,
    halo_r,
    hb_s,
    hb_r,
    pg,
    pair_ss,
    pair_rs,
    halo_ss,
    halo_rs,
    l1_ss,
    l1_rs,
    l2_ss,
    l2_rs,
    l3_ss,
    l3_rs,
    fw_ss,
    fw_rs,
    sum_ss,
    sum_rs,
    row_ready,
    edge_ready,
    cube_ready,
    far_ready,
    load,
    store,
):
    groups = chips // CUBE
    side = math.isqrt(planes)
    total = 2 * chips
    c = lax.axis_index("ctx")
    h = lax.axis_index("head")
    core = lax.rem(c, 2)
    other = 1 - core
    z = lax.div(c, 2)
    group = lax.div(z, CUBE)
    place = lax.rem(z, CUBE)
    after = (lax.rem(c + 1, total), h)
    before = (lax.rem(c + total - 1, total), h)
    partner = (2 * z + other, h)

    def in_cube(d):
        return lax.rem(place + d, CUBE)

    def cube_device(d):
        return (2 * (CUBE * group + in_cube(d)) + core, h)

    def other_group(d):
        return lax.rem(group + d, groups)

    def group_device(d):
        return (2 * (CUBE * other_group(d) + place) + core, h)

    def along(d):
        return lax.div(h, side) * side + lax.rem(lax.rem(h, side) + d, side)

    def across(d):
        return lax.rem(h + side * d, planes)

    steps = [(dx, dy) for dx in range(side) for dy in range(side) if dx + dy > 0]
    steps.sort(key=lambda step: -sum(min(d, side - d) for d in step))

    def plane_head(step):
        row = lax.rem(lax.div(h, side) + step[0], side)
        return side * row + lax.rem(lax.rem(h, side) + step[1], side)

    def chip_device(d):
        return (2 * lax.rem(z + d + chips, chips) + core, h)

    barrier = pltpu.get_barrier_semaphore()
    peers = [after, before, chip_device(1), chip_device(-1)]
    peers += [cube_device(d) for d in range(1, CUBE)]
    peers += [(c, along(d)) for d in range(1, side)]
    peers += [(c, across(d)) for d in range(1, side)]
    for peer in peers:
        pl.semaphore_signal(barrier, inc=1, device_id=peer, device_id_type=MESH)

    pairs = (
        (sta_h, sta),
        (log_h, log),
        (cp_h, cp),
        (gr_h, gr),
        (tok_h, tok),
        (cw_h, cw),
        (cb_h, cb),
        (bp_h, bp),
        (gain_h, gain),
    )
    loads = [
        pltpu.make_async_copy(src, dst, load.at[i]) for i, (src, dst) in enumerate(pairs)
    ]
    for copy in loads:
        copy.start()
    sends = []

    def send(src, dst, send_sem, recv_sem, device):
        copy = pltpu.make_async_remote_copy(
            src_ref=src,
            dst_ref=dst,
            send_sem=send_sem,
            recv_sem=recv_sem,
            device_id=device,
            device_id_type=MESH,
        )
        copy.start()
        sends.append(copy)
        return copy

    loads[0].wait()
    loads[1].wait()
    i0 = lax.broadcasted_iota(jnp.int32, (ROWS, ROWS), 0)
    i1 = lax.broadcasted_iota(jnp.int32, (ROWS, ROWS), 1)
    upper = (i0 <= i1).astype(F32)
    lower = (i0 >= i1).astype(F32)
    stk[0:HEADS] = log[...]
    stk[HEADS : 2 * HEADS] = jnp.broadcast_to(sta[...].astype(F32), (HEADS, ROWS))
    cum_row = sum_dot(stk[...], upper.astype(BF16))
    cum_col = sum_dot(stk[...], lower.astype(BF16), NT, first=False)
    cnt_row = cum_row[HEADS : HEADS + 1]
    cnt_col = cum_col[:, HEADS : HEADS + 1]
    cnt_last = cnt_col[ROWS - 1 : ROWS]
    log_col = cum_col[:, 0:HEADS]
    keep_in = (cnt_col == 0.0).astype(F32)
    keep_out = (cnt_col == cnt_last).astype(F32)
    cnt[0:8] = jnp.zeros((8, 128), F32)
    cnt[8 : 8 + ROWS] = jnp.broadcast_to(cnt_col, (ROWS, 128))
    cnt[8 + ROWS : 16 + ROWS] = jnp.broadcast_to(cnt_last, (8, 128))
    head_of = lax.broadcasted_iota(jnp.int32, (HEADS, WIDE), 0)
    lane_of = lax.broadcasted_iota(jnp.int32, (HEADS, WIDE), 1)
    pick = (lax.div(lane_of, WIDE // HEADS) == head_of).astype(F32)
    picked = pick.astype(BF16)
    win[...] = wide_dot(jnp.exp(log_col) * keep_in, picked)
    wout[...] = wide_dot(jnp.exp(log_col[ROWS - 1 : ROWS] - log_col) * keep_out, picked)
    factor = win[ROWS - 1 : ROWS, :]
    for half in range(2):
        lanes = slice(256 * half, 256 * half + 256)
        for which in range(2):
            loc[which, half, STATE : STATE + 8] = jnp.broadcast_to(factor[:, lanes], (8, 256))

    loads[2].wait()
    loads[3].wait()
    for half in range(2):
        lanes = slice(256 * half, 256 * half + 256)
        high, low = split(win[:, lanes] * gr[:, lanes].astype(F32))
        wgr[0, :, lanes] = high
        wgr[1, :, lanes] = low
        loc[1, half, 0:STATE] = dot(cp[...], high, TN) + dot(cp[...], low, TN)

    for copy in loads[4:]:
        copy.wait()
    halo_s[...] = tok[ROWS - 16 :] * keep_out[ROWS - 16 :].astype(BF16)

    def convolve(first, rows):
        for chunk in range(4):
            lanes = slice(128 * chunk, 128 * chunk + 128)
            here = cnt[8 + first : 8 + first + rows]
            value = cb[:, lanes] + cw[0:1, lanes] * ext[8 + first : 8 + first + rows, lanes]
            for k in range(1, TAPS):
                rows_at = slice(8 - k + first, 8 - k + first + rows)
                valid = (here == cnt[rows_at]).astype(F32)
                value = value + cw[k : k + 1, lanes] * ext[rows_at, lanes] * valid
            sigma = 1.0 / (1.0 + jnp.exp(-value))
            act[first : first + rows, lanes] = (value * sigma).astype(BF16)
            slope[first : first + rows, lanes] = sigma * (1.0 + value * (1.0 - sigma))

    ext[0:8] = jnp.zeros((8, WIDE), F32)
    ext[8:] = tok[...].astype(F32)
    convolve(0, ROWS)

    def local_state(rows, half):
        lanes = slice(256 * half, 256 * half + 256)
        high, low = split(wout[rows, lanes] * act[rows, lanes].astype(F32))
        wact[0, rows, lanes] = high
        wact[1, rows, lanes] = low
        return dot(bp[rows], high, TN) + dot(bp[rows], low, TN)

    for half in range(2):
        loc[0, half, 0:STATE] = local_state(slice(16, ROWS), half)

    pl.semaphore_wait(barrier, len(peers))
    halo = send(halo_s, halo_r, halo_ss.at[0], halo_rs.at[0], after)
    lowest, highest = place == 0, place == CUBE - 1
    for d in range(1, side):
        pl.semaphore_signal(row_ready, inc=1, device_id=(c, across(d)), device_id_type=MESH)
    for edge, d in ((lowest, -1), (highest, 1)):

        @pl.when(edge)
        def _():
            pl.semaphore_signal(edge_ready, inc=1, device_id=chip_device(d), device_id_type=MESH)

    halo.wait_recv()
    is_first = (c > 0).astype(F32)
    ext[0:8] = halo_r[8:16].astype(F32) * is_first
    convolve(0, 16)

    for half in range(2):
        loc[0, half, 0:STATE] += local_state(slice(0, 16), half)

    first = send(
        loc.at[core, other], rx_full.at[other], pair_ss.at[0], pair_rs.at[0], partner
    )
    second = send(loc.at[other, other], rx_half, pair_ss.at[1], pair_rs.at[1], partner)
    third = send(loc.at[core, core], rx_full.at[core], pair_ss.at[2], pair_rs.at[2], partner)

    @pl.when(lowest | highest)
    def _():
        pl.semaphore_wait(edge_ready, 1)
        for d in range(1, CUBE):
            pl.semaphore_signal(
                cube_ready, inc=1, device_id=cube_device(d), device_id_type=MESH
            )

    first.wait_recv()
    second.wait_recv()
    f_own = loc[0, core, STATE : STATE + 1]
    f_other = rx_half[STATE : STATE + 1]
    is_late = core == 1
    factor_code, factor_exponent = pack_row(f_own * f_other)
    for s in range(CUBE):
        rows, lanes = block_of(s)
        mine, e_mine = pack(rx_half[rows, lanes] + f_other[:, lanes] * loc[core, core, rows, lanes])
        yours, e_yours = pack(
            loc[other, core, rows, lanes] + f_own[:, lanes] * rx_full[core, rows, lanes]
        )
        chip[s, pl.ds(pl.multiple_of(64 * core, 64), 64)] = mine
        chip[s, pl.ds(pl.multiple_of(64 * other, 64), 64)] = yours
        chip[s, 128:144] = tile_of(
            jnp.where(is_late, e_yours, e_mine),
            jnp.where(is_late, e_mine, e_yours),
            factor_exponent[:, lanes],
            factor_code[:, lanes],
        )

    l1[place] = chip[place]
    ups = []
    for d in range(1, CUBE):
        ups.append(
            send(chip.at[in_cube(d)], l1.at[place], l1_ss.at[d - 1], l1_rs.at[d - 1], cube_device(d))
        )

    inside = jnp.logical_not(lowest | highest)
    middle = (group > 0) & (group < groups - 1)
    upper_half = group >= 2
    pl.semaphore_wait(cube_ready, 1 + inside.astype(jnp.int32))

    @pl.when(middle)
    def _():
        pl.semaphore_signal(far_ready, inc=1, device_id=group_device(1), device_id_type=MESH)

    gain_wide = exact_dot(jnp.broadcast_to(gain[...], (8, HEADS)), pick)[0:1]
    scores = dot(bp[...], cp[...], NT)
    bias = jnp.where((i0 <= i1) & (cnt_col == cnt_row), 0.0, -1e30)
    even = lax.broadcasted_iota(jnp.int32, (ROWS, 128), 1) < 64

    def intra(pair, begin):
        lanes = slice(128 * pair, 128 * pair + 128)
        parts = []
        for head in (2 * pair, 2 * pair + 1):
            decay = jnp.exp(cum_row[head : head + 1] - cum_col[:, head : head + 1] + bias)
            mixed = decay * scores
            parts.append(dot(mixed.astype(BF16), gr[:, lanes]))
            mine = even if head % 2 == 0 else ~even
            rows = jnp.where(mine, act[:, lanes].astype(F32), 0.0).astype(BF16)
            inner = dot(rows, gr[:, lanes], NT)
            if begin and head % 2 == 0:
                sg[...] = decay * inner
            else:
                sg[...] += decay * inner
            product = mixed * inner
            rowtot[head : head + 1] = jnp.sum(product, axis=0, keepdims=True)
            xcol[:, head : head + 1] = jnp.sum(product, axis=1, keepdims=True)
        agr[:, lanes] = jnp.where(even, parts[0], parts[1]) + gain_wide[:, lanes] * gr[
            :, lanes
        ].astype(F32)

    intra(0, True)
    intra(1, False)

    for copy in ups:
        copy.wait_recv()

    def unpack_slot(ref, j, arrays):
        tile = ref[j, 64 * arrays : 64 * arrays + 16].astype(jnp.int32).astype(F32)
        values = [
            unpack(ref[j, 64 * i : 64 * i + 64], tile[i : i + 1]) for i in range(arrays)
        ]
        factor = tile[arrays + 1 : arrays + 2] * scale_of(tile[arrays : arrays + 1] - 14.0)
        return values, factor

    slots = [unpack_slot(l1, j, 2) for j in range(CUBE)]

    def prefixes():
        values, factors = [jnp.zeros((64, 128), F32)], [jnp.ones((1, 128), F32)]
        for (state, _), f in slots:
            values.append(state + f * values[-1])
            factors.append(f * factors[-1])
        return values, factors

    def suffixes():
        values, factors = [jnp.zeros((64, 128), F32)], [jnp.ones((1, 128), F32)]
        for (_, adjoint), f in reversed(slots):
            values.append(adjoint + f * values[-1])
            factors.append(f * factors[-1])
        return values[::-1], factors[::-1]

    down, down_f = prefixes()
    up, up_f = suffixes()
    factor_code, factor_exponent = pack_row(down_f[CUBE])
    for kind, total_here in enumerate((down[CUBE], up[0])):
        coded, exponent = pack(total_here)
        out2[kind, 0:64] = coded
        out2[kind, 64:80] = tile_of(exponent, factor_exponent, factor_code)
    crosses = []
    for i, d in enumerate((1, groups - 1)):
        kind = (other_group(d) < group).astype(jnp.int32)
        crosses.append(
            send(out2.at[kind], l2.at[group], l2_ss.at[i], l2_rs.at[i], group_device(d))
        )

    def to_group(src, slot, i, d):
        return pltpu.make_async_remote_copy(
            src_ref=src,
            dst_ref=l2.at[slot],
            send_sem=l2_ss.at[i],
            recv_sem=l2_rs.at[2],
            device_id=group_device(d),
            device_id_type=MESH,
        )

    relay = to_group(l2.at[other_group(groups - 1)], other_group(groups - 1), 2, 1)
    direct = to_group(out2.at[1], group, 3, 2)

    @pl.when(upper_half)
    def _():
        pl.semaphore_wait(far_ready, 1)
        direct.start()

    intra(2, False)
    intra(3, False)

    crosses[0].wait_recv()

    @pl.when(middle)
    def _():
        relay.start()

    crosses[1].wait_recv()
    relay.wait_recv()
    totals = [unpack_slot(l2, u, 1) for u in range(groups)]
    from_before = jnp.zeros((64, 128), F32)
    for u in range(groups):
        (value,), f = totals[u]
        from_before = jnp.where(u < group, value + f * from_before, from_before)
    from_after = jnp.zeros((64, 128), F32)
    for u in reversed(range(groups)):
        (value,), f = totals[u]
        from_after = jnp.where(u > group, value + f * from_after, from_after)
    for j in range(CUBE):
        state, e_state = pack(down[j] + down_f[j] * from_before)
        adjoint, e_adjoint = pack(up[j + 1] + up_f[j + 1] * from_after)
        o3[j, 0:64] = state
        o3[j, 64:128] = adjoint
        o3[j, 128:144] = tile_of(e_state, e_adjoint)
    full[core, place] = o3[place]
    forwards = []
    backs = []
    for d in range(1, CUBE):
        backs.append(
            send(
                o3.at[in_cube(d)],
                full.at[core, place],
                l3_ss.at[d - 1],
                l3_rs.at[d - 1],
                cube_device(d),
            )
        )
    here = full.at[core, place]
    forwards.append(send(here, here, fw_ss.at[0], fw_rs.at[0], partner))

    high, low = split(sg[...])
    rs_src[:, 0:STATE] = dot(high, cp[...]) + dot(low, cp[...])
    rs_src[:, STATE:] = dot(high, bp[...], TN) + dot(low, bp[...], TN)

    for d in range(1, CUBE):
        backs[d - 1].wait_recv()
        slot = full.at[core, in_cube(CUBE - d)]
        forwards.append(send(slot, slot, fw_ss.at[d], fw_rs.at[d], partner))
    third.wait_recv()
    for copy in forwards:
        copy.wait_recv()

    def incoming(half, which):
        blocks = []
        for s in range(CUBE):
            tile = full[half, s, 128:144].astype(jnp.int32).astype(F32)
            blocks.append(
                unpack(full[half, s, 64 * which : 64 * which + 64], tile[which : which + 1])
            )
        top = jnp.concatenate(blocks[0:2], axis=1)
        return jnp.concatenate([top, jnp.concatenate(blocks[2:4], axis=1)], axis=0)

    late = (core == 1).astype(F32)
    early = 1.0 - late
    state_in, adjoint_in, end_row = [], [], []
    for half in range(2):
        f_other = rx_full[half, STATE : STATE + 1]
        received = rx_full[half, 0:STATE]
        f_own = loc[0, half, STATE : STATE + 1]
        wide = incoming(half, 0)
        state = late * received + (late * f_other + early) * wide
        wide = incoming(half, 1)
        adjoint = early * received + (early * f_other + late) * wide
        state_out = loc[0, half, 0:STATE] + f_own * state
        end_row.append(jnp.sum(adjoint * state_out, axis=0, keepdims=True))
        state_in.append(split(state))
        adjoint_in.append(split(adjoint))

    b_part = rs_src[:, 0:STATE]
    c_part = rs_src[:, STATE:]
    for half in range(2):
        lanes = slice(256 * half, 256 * half + 256)
        for left, right in ((0, 0), (1, 0), (0, 1)):
            b_part = b_part + dot(wact[left, :, lanes], adjoint_in[half][right], NT)
            c_part = c_part + dot(wgr[left, :, lanes], state_in[half][right], NT)
    rs_out[:, 0:STATE] = b_part.astype(BF16)
    rs_out[:, STATE:] = c_part.astype(BF16)
    keep = pltpu.make_async_copy(
        rs_out.at[pl.ds(pl.multiple_of(16 * h, 16), 16)], sum_h.at[h], store.at[4]
    )
    keep.start()
    pl.semaphore_wait(row_ready, side - 1)
    sums = []
    for i, step in enumerate(steps):
        target = plane_head(step)
        rows = pl.ds(pl.multiple_of(16 * target, 16), 16)
        sums.append(
            send(rs_out.at[rows], sum_h.at[h], sum_ss.at[i], sum_rs.at[i], (c, target))
        )

    inter = jnp.zeros((HEADS, ROWS), F32)
    for half in range(2):
        lanes = slice(256 * half, 256 * half + 256)
        after_part = wout[:, lanes] * dot(bp[...], adjoint_in[half][0])
        before_part = win[:, lanes] * dot(cp[...], state_in[half][0])
        pg[0:ROWS, lanes] = (agr[:, lanes] + after_part) * slope[:, lanes]
        difference = before_part * gr[:, lanes].astype(F32) - after_part * act[:, lanes].astype(F32)
        inter = inter + exact_dot(pick[:, lanes], difference, NT)
    hb_s[...] = pg[0:8] * keep_in[0:8]
    back = send(hb_s, hb_r, halo_ss.at[1], halo_rs.at[1], before)

    ends = jnp.sum(pick * jnp.concatenate(end_row, axis=1), axis=1, keepdims=True)
    cum_total = rowtot[...] + inter - xcol[...].T[0:HEADS]
    o_dec[...] = exact_dot(cum_total, lower) + ends
    stores = [pltpu.make_async_copy(o_dec, dec_h, store.at[5])]
    stores[0].start()

    back.wait_recv()
    is_last = (c < total - 1).astype(F32)
    pg[ROWS:] = hb_r[...] * is_last
    for chunk in range(4):
        lanes = slice(128 * chunk, 128 * chunk + 128)
        value = cw[0:1, lanes] * pg[0:ROWS, lanes]
        for k in range(1, TAPS):
            valid = (cnt[8 + k : 8 + k + ROWS] == cnt[8 : 8 + ROWS]).astype(F32)
            value = value + cw[k : k + 1, lanes] * pg[k : k + ROWS, lanes] * valid
        o_in[:, lanes] = value
        stores.append(pltpu.make_async_copy(o_in.at[:, lanes], in_h.at[:, lanes], store.at[chunk]))
        stores[-1].start()

    for copy in sums:
        copy.wait_recv()
    stores.append(keep)
    for copy in stores:
        copy.wait()

    for copy in sends:
        copy.wait_send()

    @pl.when(middle)
    def _():
        relay.wait_send()

    @pl.when(upper_half)
    def _():
        direct.wait_send()


def finish(a_in, a_sum, a_dec, o_in, o_b, o_c, o_dec, wide, sums, both, decay, load, store):
    def go(i, src, dst, sem):
        return pltpu.make_async_copy(src, dst, sem.at[i])

    half = ROWS // 2
    triples = [(a_sum, sums, None)]
    triples += [(a_in.at[p], wide.at[p], o_in.at[p]) for p in (pl.ds(0, half), pl.ds(half, half))]
    triples += [(a_dec, decay, o_dec)]
    loads = [go(i, src, mid, load) for i, (src, mid, _) in enumerate(triples)]
    stores = [go(0, both.at[0], o_b, store)]
    stores += [go(i, mid, dst, store) for i, (_, mid, dst) in enumerate(triples) if i > 0]
    stores += [go(4, both.at[1], o_c, store)]
    for copy in loads:
        copy.start()
    for i in range(1, 4):
        loads[i].wait()
        stores[i].start()
    loads[0].wait()
    total = sums[0].astype(F32)
    for j in range(1, sums.shape[0]):
        total = total + sums[j].astype(F32)
    both[0] = total[:, 0:STATE]
    both[1] = total[:, STATE:]
    stores[0].start()
    stores[4].start()
    for copy in stores:
        copy.wait()


def body(tokens_in, starts, log_decay, b_proj, c_proj, out_grad, conv_weight, conv_bias, skip_gain):
    chips = lax.axis_size("ctx") // 2
    planes = lax.axis_size("head")
    groups = chips // CUBE
    own = ROWS // planes
    vmem = pltpu.VMEM
    dma = pltpu.SemaphoreType.DMA
    in_grad, sums, decay_grad = pl.pallas_call(
        functools.partial(kernel, chips, planes),
        out_shape=(
            jax.ShapeDtypeStruct((ROWS, WIDE), F32),
            jax.ShapeDtypeStruct((planes, own, 2 * STATE), BF16),
            jax.ShapeDtypeStruct((HEADS, ROWS), F32),
        ),
        in_specs=[pl.BlockSpec(memory_space=pltpu.HBM)] * 9,
        out_specs=[pl.BlockSpec(memory_space=pltpu.HBM)] * 3,
        scratch_shapes=[
            vmem((ROWS, WIDE), F32),
            vmem((HEADS, ROWS), F32),
            vmem((ROWS, WIDE), BF16),
            vmem((1, ROWS), jnp.int32),
            vmem((HEADS, ROWS), F32),
            vmem((ROWS, STATE), BF16),
            vmem((ROWS, STATE), BF16),
            vmem((ROWS, WIDE), BF16),
            vmem((TAPS, WIDE), F32),
            vmem((1, WIDE), F32),
            vmem((1, HEADS), F32),
            vmem((8 + ROWS, WIDE), F32),
            vmem((16 + ROWS, 128), F32),
            vmem((2 * HEADS, ROWS), F32),
            vmem((ROWS, WIDE), BF16),
            vmem((ROWS, WIDE), F32),
            vmem((2, ROWS, WIDE), BF16),
            vmem((2, ROWS, WIDE), BF16),
            vmem((ROWS, WIDE), F32),
            vmem((ROWS, WIDE), F32),
            vmem((ROWS, WIDE), F32),
            vmem((ROWS, ROWS), F32),
            vmem((HEADS, ROWS), F32),
            vmem((ROWS, 128), F32),
            vmem((2, 2, STATE + 8, 256), F32),
            vmem((2, STATE + 8, 256), F32),
            vmem((STATE + 8, 256), F32),
            vmem((CUBE, 144, 128), jnp.int16),
            vmem((CUBE, 144, 128), jnp.int16),
            vmem((2, 80, 128), jnp.int16),
            vmem((groups, 80, 128), jnp.int16),
            vmem((CUBE, 144, 128), jnp.int16),
            vmem((2, CUBE, 144, 128), jnp.int16),
            vmem((ROWS, 2 * STATE), F32),
            vmem((ROWS, 2 * STATE), BF16),
            vmem((16, WIDE), BF16),
            vmem((16, WIDE), BF16),
            vmem((8, WIDE), F32),
            vmem((8, WIDE), F32),
            vmem((8 + ROWS, WIDE), F32),
            dma((3,)),
            dma((3,)),
            dma((2,)),
            dma((2,)),
            dma((CUBE - 1,)),
            dma((CUBE - 1,)),
            dma((4,)),
            dma((3,)),
            dma((CUBE - 1,)),
            dma((CUBE - 1,)),
            dma((CUBE,)),
            dma((CUBE,)),
            dma((max(planes - 1, 1),)),
            dma((max(planes - 1, 1),)),
            pltpu.SemaphoreType.REGULAR,
            pltpu.SemaphoreType.REGULAR,
            pltpu.SemaphoreType.REGULAR,
            pltpu.SemaphoreType.REGULAR,
            dma((9,)),
            dma((6,)),
        ],
        compiler_params=pltpu.CompilerParams(
            collective_id=0, has_side_effects=True, vmem_limit_bytes=63 * 1024 * 1024
        ),
        name="layer",
    )(
        tokens_in,
        starts.reshape(1, ROWS),
        log_decay,
        b_proj,
        c_proj,
        out_grad,
        conv_weight,
        conv_bias.reshape(1, WIDE),
        skip_gain.reshape(1, HEADS),
    )
    in_grad, b_grad, c_grad, decay_grad = pl.pallas_call(
        finish,
        out_shape=(
            jax.ShapeDtypeStruct((ROWS, WIDE), F32),
            jax.ShapeDtypeStruct((own, STATE), F32),
            jax.ShapeDtypeStruct((own, STATE), F32),
            jax.ShapeDtypeStruct((HEADS, ROWS), F32),
        ),
        in_specs=[pl.BlockSpec(memory_space=pl.ANY)] * 3,
        out_specs=[pl.BlockSpec(memory_space=pltpu.HBM)] * 4,
        scratch_shapes=[
            vmem((ROWS, WIDE), F32),
            vmem((planes, own, 2 * STATE), BF16),
            vmem((2, own, STATE), F32),
            vmem((HEADS, ROWS), F32),
            dma((4,)),
            dma((5,)),
        ],
        compiler_params=pltpu.CompilerParams(vmem_limit_bytes=63 * 1024 * 1024),
        name="finish",
    )(in_grad, sums, decay_grad)
    return (in_grad, b_grad, c_grad, decay_grad)


def solution(mesh):
    placed = (
        P("ctx", "head"),
        P("ctx"),
        P("head", "ctx"),
        P("ctx", None),
        P("ctx", None),
        P("ctx", "head"),
        P(None, "head"),
        P("head"),
        P("head"),
    )
    return jax.shard_map(
        body,
        mesh=mesh,
        in_specs=placed,
        out_specs=(
            P("ctx", "head"),
            P(("ctx", "head"), None),
            P(("ctx", "head"), None),
            P("head", "ctx"),
        ),
        check_vma=False,
    )
```

```python
import functools
import math

import jax
import jax.numpy as jnp
from jax import lax
from jax.experimental import pallas as pl
from jax.experimental.pallas import tpu as pltpu
from jax.sharding import PartitionSpec as P

MESH = pl.DeviceIdType.MESH
F32 = jnp.float32
BF16 = jnp.bfloat16
HIGHEST = lax.Precision.HIGHEST

ROWS = 256
HEADS = 8
WIDE = 512
STATE = 128
TAPS = 4
CUBE = 4

NN = (((1,), (0,)), ((), ()))
NT = (((1,), (1,)), ((), ()))
TN = (((0,), (0,)), ((), ()))


def dot(a, b, dims=NN):
    return lax.dot_general(a, b, dims, preferred_element_type=F32)


def exact_dot(a, b, dims=NN):
    return lax.dot_general(a, b, dims, precision=HIGHEST, preferred_element_type=F32)


def split(x):
    high = x.astype(BF16)
    return high, (x - high.astype(F32)).astype(BF16)


def sum_dot(x, ones, dims=NN, first=True):
    high = x.astype(BF16)
    rest = x - high.astype(F32)
    middle = rest.astype(BF16)
    low = (rest - middle.astype(F32)).astype(BF16)
    parts = [dot(p, ones, dims) if first else dot(ones, p, dims) for p in (high, middle, low)]
    return parts[0] + (parts[1] + parts[2])


def wide_dot(x, y, dims=NN):
    high, low = split(x)
    return dot(high, y, dims) + dot(low, y, dims)


def scale_of(exponent):
    return jnp.exp2(exponent.astype(F32))


def exponent_of(largest):
    bits = jnp.floor(jnp.log(jnp.maximum(largest, 1e-36)) * 1.4426950408889634) + 1.0
    return jnp.clip(bits, -100.0, 100.0)


def code(x, exponent):
    return jnp.floor(x * scale_of(14.0 - exponent) + 0.5).astype(jnp.int32)


def pack(x):
    exponent = exponent_of(jnp.max(jnp.abs(x), axis=0, keepdims=True))
    return code(x, exponent).astype(jnp.int16), exponent


def pack_row(x):
    exponent = exponent_of(x)
    return code(x, exponent).astype(F32), exponent


def unpack(x, exponent):
    return x.astype(jnp.int32).astype(F32) * scale_of(exponent - 14.0)


def tile_of(*rows):
    row_of = lax.broadcasted_iota(jnp.int32, (16, 128), 0)
    tile = jnp.zeros((16, 128), F32)
    for i, row in enumerate(rows):
        tile = jnp.where(row_of == i, row, tile)
    return tile.astype(jnp.int32).astype(jnp.int16)


def block_of(place):
    row, lane = 64 * (place // 2), 128 * (place % 2)
    return slice(row, row + 64), slice(lane, lane + 128)


def kernel(
    chips,
    planes,
    tok_h,
    sta_h,
    log_h,
    bp_h,
    cp_h,
    gr_h,
    cw_h,
    cb_h,
    gain_h,
    in_h,
    sum_h,
    dec_h,
    o_in,
    o_dec,
    tok,
    sta,
    log,
    bp,
    cp,
    gr,
    cw,
    cb,
    gain,
    ext,
    cnt,
    stk,
    act,
    slope,
    wact,
    wgr,
    win,
    wout,
    agr,
    sg,
    rowtot,
    xcol,
    loc,
    rx_full,
    rx_half,
    chip,
    l1,
    out2,
    l2,
    o3,
    full,
    into,
    rs_src,
    rs_out,
    halo_s,
    halo_r,
    hb_s,
    hb_r,
    pg,
    pair_ss,
    pair_rs,
    halo_ss,
    halo_rs,
    l1_ss,
    l1_rs,
    l2_ss,
    l2_rs,
    l3_ss,
    l3_rs,
    fw_ss,
    fw_rs,
    sum_ss,
    sum_rs,
    row_ready,
    edge_ready,
    cube_ready,
    far_ready,
    load,
    store,
):
    groups = chips // CUBE
    side = math.isqrt(planes)
    total = 2 * chips
    c = lax.axis_index("ctx")
    h = lax.axis_index("head")
    core = lax.rem(c, 2)
    other = 1 - core
    z = lax.div(c, 2)
    group = lax.div(z, CUBE)
    place = lax.rem(z, CUBE)
    after = (lax.rem(c + 1, total), h)
    before = (lax.rem(c + total - 1, total), h)
    partner = (2 * z + other, h)

    def in_cube(d):
        return lax.rem(place + d, CUBE)

    def cube_device(d):
        return (2 * (CUBE * group + in_cube(d)) + core, h)

    def other_group(d):
        return lax.rem(group + d, groups)

    def group_device(d):
        return (2 * (CUBE * other_group(d) + place) + core, h)

    def along(d):
        return lax.div(h, side) * side + lax.rem(lax.rem(h, side) + d, side)

    def across(d):
        return lax.rem(h + side * d, planes)

    steps = [(dx, dy) for dx in range(side) for dy in range(side) if dx + dy > 0]
    steps.sort(key=lambda step: -sum(min(d, side - d) for d in step))

    def plane_head(step):
        row = lax.rem(lax.div(h, side) + step[0], side)
        return side * row + lax.rem(lax.rem(h, side) + step[1], side)

    def chip_device(d):
        return (2 * lax.rem(z + d + chips, chips) + core, h)

    barrier = pltpu.get_barrier_semaphore()
    peers = [after, before, chip_device(1), chip_device(-1)]
    peers += [cube_device(d) for d in range(1, CUBE)]
    peers += [(c, along(d)) for d in range(1, side)]
    peers += [(c, across(d)) for d in range(1, side)]
    for peer in peers:
        pl.semaphore_signal(barrier, inc=1, device_id=peer, device_id_type=MESH)

    pairs = (
        (sta_h, sta),
        (log_h, log),
        (cp_h, cp),
        (gr_h, gr),
        (tok_h, tok),
        (cw_h, cw),
        (cb_h, cb),
        (bp_h, bp),
        (gain_h, gain),
    )
    loads = [
        pltpu.make_async_copy(src, dst, load.at[i]) for i, (src, dst) in enumerate(pairs)
    ]
    for copy in loads:
        copy.start()
    sends = []

    def send(src, dst, send_sem, recv_sem, device):
        copy = pltpu.make_async_remote_copy(
            src_ref=src,
            dst_ref=dst,
            send_sem=send_sem,
            recv_sem=recv_sem,
            device_id=device,
            device_id_type=MESH,
        )
        copy.start()
        sends.append(copy)
        return copy

    loads[0].wait()
    loads[1].wait()
    i0 = lax.broadcasted_iota(jnp.int32, (ROWS, ROWS), 0)
    i1 = lax.broadcasted_iota(jnp.int32, (ROWS, ROWS), 1)
    upper = (i0 <= i1).astype(F32)
    lower = (i0 >= i1).astype(F32)
    stk[0:HEADS] = log[...]
    stk[HEADS : 2 * HEADS] = jnp.broadcast_to(sta[...].astype(F32), (HEADS, ROWS))
    cum_row = sum_dot(stk[...], upper.astype(BF16))
    cum_col = sum_dot(stk[...], lower.astype(BF16), NT, first=False)
    cnt_row = cum_row[HEADS : HEADS + 1]
    cnt_col = cum_col[:, HEADS : HEADS + 1]
    cnt_last = cnt_col[ROWS - 1 : ROWS]
    log_col = cum_col[:, 0:HEADS]
    keep_in = (cnt_col == 0.0).astype(F32)
    keep_out = (cnt_col == cnt_last).astype(F32)
    cnt[0:8] = jnp.zeros((8, 128), F32)
    cnt[8 : 8 + ROWS] = jnp.broadcast_to(cnt_col, (ROWS, 128))
    cnt[8 + ROWS : 16 + ROWS] = jnp.broadcast_to(cnt_last, (8, 128))
    head_of = lax.broadcasted_iota(jnp.int32, (HEADS, WIDE), 0)
    lane_of = lax.broadcasted_iota(jnp.int32, (HEADS, WIDE), 1)
    pick = (lax.div(lane_of, WIDE // HEADS) == head_of).astype(F32)
    picked = pick.astype(BF16)
    win[...] = wide_dot(jnp.exp(log_col) * keep_in, picked)
    wout[...] = wide_dot(jnp.exp(log_col[ROWS - 1 : ROWS] - log_col) * keep_out, picked)
    factor = win[ROWS - 1 : ROWS, :]
    for half in range(2):
        lanes = slice(256 * half, 256 * half + 256)
        for which in range(2):
            loc[which, half, STATE : STATE + 8] = jnp.broadcast_to(factor[:, lanes], (8, 256))

    loads[2].wait()
    loads[3].wait()
    for half in range(2):
        lanes = slice(256 * half, 256 * half + 256)
        high, low = split(win[:, lanes] * gr[:, lanes].astype(F32))
        wgr[0, :, lanes] = high
        wgr[1, :, lanes] = low
        loc[1, half, 0:STATE] = dot(cp[...], high, TN) + dot(cp[...], low, TN)

    for copy in loads[4:]:
        copy.wait()
    halo_s[...] = tok[ROWS - 16 :] * keep_out[ROWS - 16 :].astype(BF16)

    def convolve(first, rows):
        for chunk in range(4):
            lanes = slice(128 * chunk, 128 * chunk + 128)
            here = cnt[8 + first : 8 + first + rows]
            value = cb[:, lanes] + cw[0:1, lanes] * ext[8 + first : 8 + first + rows, lanes]
            for k in range(1, TAPS):
                rows_at = slice(8 - k + first, 8 - k + first + rows)
                valid = (here == cnt[rows_at]).astype(F32)
                value = value + cw[k : k + 1, lanes] * ext[rows_at, lanes] * valid
            sigma = 1.0 / (1.0 + jnp.exp(-value))
            act[first : first + rows, lanes] = (value * sigma).astype(BF16)
            slope[first : first + rows, lanes] = sigma * (1.0 + value * (1.0 - sigma))

    ext[0:8] = jnp.zeros((8, WIDE), F32)
    ext[8:] = tok[...].astype(F32)
    convolve(0, ROWS)

    def local_state(rows, half):
        lanes = slice(256 * half, 256 * half + 256)
        high, low = split(wout[rows, lanes] * act[rows, lanes].astype(F32))
        wact[0, rows, lanes] = high
        wact[1, rows, lanes] = low
        return dot(bp[rows], high, TN) + dot(bp[rows], low, TN)

    for half in range(2):
        loc[0, half, 0:STATE] = local_state(slice(16, ROWS), half)

    pl.semaphore_wait(barrier, len(peers))
    halo = send(halo_s, halo_r, halo_ss.at[0], halo_rs.at[0], after)
    lowest, highest = place == 0, place == CUBE - 1
    for d in range(1, side):
        pl.semaphore_signal(row_ready, inc=1, device_id=(c, across(d)), device_id_type=MESH)
    for edge, d in ((lowest, -1), (highest, 1)):

        @pl.when(edge)
        def _():
            pl.semaphore_signal(edge_ready, inc=1, device_id=chip_device(d), device_id_type=MESH)

    halo.wait_recv()
    is_first = (c > 0).astype(F32)
    ext[0:8] = halo_r[8:16].astype(F32) * is_first
    convolve(0, 16)

    for half in range(2):
        loc[0, half, 0:STATE] += local_state(slice(0, 16), half)

    first = send(
        loc.at[core, other], rx_full.at[other], pair_ss.at[0], pair_rs.at[0], partner
    )
    second = send(loc.at[other, other], rx_half, pair_ss.at[1], pair_rs.at[1], partner)
    third = send(loc.at[core, core], rx_full.at[core], pair_ss.at[2], pair_rs.at[2], partner)

    @pl.when(lowest | highest)
    def _():
        pl.semaphore_wait(edge_ready, 1)
        for d in range(1, CUBE):
            pl.semaphore_signal(
                cube_ready, inc=1, device_id=cube_device(d), device_id_type=MESH
            )

    first.wait_recv()
    second.wait_recv()
    f_own = loc[0, core, STATE : STATE + 1]
    f_other = rx_half[STATE : STATE + 1]
    is_late = core == 1
    factor_code, factor_exponent = pack_row(f_own * f_other)
    for s in range(CUBE):
        rows, lanes = block_of(s)
        mine, e_mine = pack(rx_half[rows, lanes] + f_other[:, lanes] * loc[core, core, rows, lanes])
        yours, e_yours = pack(
            loc[other, core, rows, lanes] + f_own[:, lanes] * rx_full[core, rows, lanes]
        )
        chip[s, pl.ds(pl.multiple_of(64 * core, 64), 64)] = mine
        chip[s, pl.ds(pl.multiple_of(64 * other, 64), 64)] = yours
        chip[s, 128:144] = tile_of(
            jnp.where(is_late, e_yours, e_mine),
            jnp.where(is_late, e_mine, e_yours),
            factor_exponent[:, lanes],
            factor_code[:, lanes],
        )

    l1[place] = chip[place]
    ups = []
    for d in range(1, CUBE):
        ups.append(
            send(chip.at[in_cube(d)], l1.at[place], l1_ss.at[d - 1], l1_rs.at[d - 1], cube_device(d))
        )

    inside = jnp.logical_not(lowest | highest)
    middle = (group > 0) & (group < groups - 1)
    upper_half = group >= 2
    pl.semaphore_wait(cube_ready, 1 + inside.astype(jnp.int32))

    @pl.when(middle)
    def _():
        pl.semaphore_signal(far_ready, inc=1, device_id=group_device(1), device_id_type=MESH)

    gain_wide = exact_dot(jnp.broadcast_to(gain[...], (8, HEADS)), pick)[0:1]
    scores = dot(bp[...], cp[...], NT)
    bias = jnp.where((i0 <= i1) & (cnt_col == cnt_row), 0.0, -1e30)
    even = lax.broadcasted_iota(jnp.int32, (ROWS, 128), 1) < 64

    def intra(pair, begin):
        lanes = slice(128 * pair, 128 * pair + 128)
        parts = []
        for head in (2 * pair, 2 * pair + 1):
            decay = jnp.exp(cum_row[head : head + 1] - cum_col[:, head : head + 1] + bias)
            mixed = decay * scores
            parts.append(dot(mixed.astype(BF16), gr[:, lanes]))
            mine = even if head % 2 == 0 else ~even
            rows = jnp.where(mine, act[:, lanes].astype(F32), 0.0).astype(BF16)
            inner = dot(rows, gr[:, lanes], NT)
            if begin and head % 2 == 0:
                sg[...] = decay * inner
            else:
                sg[...] += decay * inner
            product = mixed * inner
            rowtot[head : head + 1] = jnp.sum(product, axis=0, keepdims=True)
            xcol[:, head : head + 1] = jnp.sum(product, axis=1, keepdims=True)
        agr[:, lanes] = jnp.where(even, parts[0], parts[1]) + gain_wide[:, lanes] * gr[
            :, lanes
        ].astype(F32)

    intra(0, True)
    intra(1, False)

    for copy in ups:
        copy.wait_recv()

    def unpack_slot(ref, j, arrays):
        tile = ref[j, 64 * arrays : 64 * arrays + 16].astype(jnp.int32).astype(F32)
        values = [
            unpack(ref[j, 64 * i : 64 * i + 64], tile[i : i + 1]) for i in range(arrays)
        ]
        factor = tile[arrays + 1 : arrays + 2] * scale_of(tile[arrays : arrays + 1] - 14.0)
        return values, factor

    slots = [unpack_slot(l1, j, 2) for j in range(CUBE)]

    def prefixes():
        values, factors = [jnp.zeros((64, 128), F32)], [jnp.ones((1, 128), F32)]
        for (state, _), f in slots:
            values.append(state + f * values[-1])
            factors.append(f * factors[-1])
        return values, factors

    def suffixes():
        values, factors = [jnp.zeros((64, 128), F32)], [jnp.ones((1, 128), F32)]
        for (_, adjoint), f in reversed(slots):
            values.append(adjoint + f * values[-1])
            factors.append(f * factors[-1])
        return values[::-1], factors[::-1]

    down, down_f = prefixes()
    up, up_f = suffixes()
    factor_code, factor_exponent = pack_row(down_f[CUBE])
    for kind, total_here in enumerate((down[CUBE], up[0])):
        coded, exponent = pack(total_here)
        out2[kind, 0:64] = coded
        out2[kind, 64:80] = tile_of(exponent, factor_exponent, factor_code)
    crosses = []
    for i, d in enumerate((1, groups - 1)):
        kind = (other_group(d) < group).astype(jnp.int32)
        crosses.append(
            send(out2.at[kind], l2.at[group], l2_ss.at[i], l2_rs.at[i], group_device(d))
        )

    def to_group(src, slot, i, d):
        return pltpu.make_async_remote_copy(
            src_ref=src,
            dst_ref=l2.at[slot],
            send_sem=l2_ss.at[i],
            recv_sem=l2_rs.at[2],
            device_id=group_device(d),
            device_id_type=MESH,
        )

    relay = to_group(l2.at[other_group(groups - 1)], other_group(groups - 1), 2, 1)
    direct = to_group(out2.at[1], group, 3, 2)

    @pl.when(upper_half)
    def _():
        pl.semaphore_wait(far_ready, 1)
        direct.start()

    intra(2, False)
    intra(3, False)

    crosses[0].wait_recv()

    @pl.when(middle)
    def _():
        relay.start()

    crosses[1].wait_recv()
    relay.wait_recv()
    totals = [unpack_slot(l2, u, 1) for u in range(groups)]
    from_before = jnp.zeros((64, 128), F32)
    for u in range(groups):
        (value,), f = totals[u]
        from_before = jnp.where(u < group, value + f * from_before, from_before)
    from_after = jnp.zeros((64, 128), F32)
    for u in reversed(range(groups)):
        (value,), f = totals[u]
        from_after = jnp.where(u > group, value + f * from_after, from_after)
    for j in range(CUBE):
        state, e_state = pack(down[j] + down_f[j] * from_before)
        adjoint, e_adjoint = pack(up[j + 1] + up_f[j + 1] * from_after)
        o3[j, 0:64] = state
        o3[j, 64:128] = adjoint
        o3[j, 128:144] = tile_of(e_state, e_adjoint)
    full[core, place] = o3[place]
    forwards = []
    backs = []
    for d in range(1, CUBE):
        backs.append(
            send(
                o3.at[in_cube(d)],
                full.at[core, place],
                l3_ss.at[d - 1],
                l3_rs.at[d - 1],
                cube_device(d),
            )
        )
    here = full.at[core, place]
    forwards.append(send(here, here, fw_ss.at[0], fw_rs.at[0], partner))

    high, low = split(sg[...])
    rs_src[:, 0:STATE] = dot(high, cp[...]) + dot(low, cp[...])
    rs_src[:, STATE:] = dot(high, bp[...], TN) + dot(low, bp[...], TN)

    for d in range(1, CUBE):
        backs[d - 1].wait_recv()
        slot = full.at[core, in_cube(CUBE - d)]
        forwards.append(send(slot, slot, fw_ss.at[d], fw_rs.at[d], partner))
    third.wait_recv()

    def incoming(half, which):
        blocks = []
        for s in range(CUBE):
            tile = full[half, s, 128:144].astype(jnp.int32).astype(F32)
            blocks.append(
                unpack(full[half, s, 64 * which : 64 * which + 64], tile[which : which + 1])
            )
        top = jnp.concatenate(blocks[0:2], axis=1)
        return jnp.concatenate([top, jnp.concatenate(blocks[2:4], axis=1)], axis=0)

    late = (core == 1).astype(F32)
    early = 1.0 - late

    for half in (core, other):
        if half is other:
            for copy in forwards:
                copy.wait_recv()
        lanes = pl.ds(pl.multiple_of(256 * half, 256), 256)
        f_other = rx_full[half, STATE : STATE + 1]
        received = rx_full[half, 0:STATE]
        state = late * received + (late * f_other + early) * incoming(half, 0)
        adjoint = early * received + (early * f_other + late) * incoming(half, 1)
        into[0, half] = state
        into[1, half] = adjoint
        for which, value, rows in ((0, adjoint, wact), (1, state, wgr)):
            high, low = split(value)
            both = dot(rows[0, :, lanes], jnp.concatenate([high, low], axis=0), NT)
            part = both[:, 0:STATE] + both[:, STATE:] + dot(rows[1, :, lanes], high, NT)
            columns = slice(STATE * which, STATE * which + STATE)
            if half is other:
                rs_out[:, columns] = (rs_src[:, columns] + part).astype(BF16)
            else:
                rs_src[:, columns] += part

    keep = pltpu.make_async_copy(
        rs_out.at[pl.ds(pl.multiple_of(16 * h, 16), 16)], sum_h.at[h], store.at[4]
    )
    keep.start()
    pl.semaphore_wait(row_ready, side - 1)
    sums = []
    for i, step in enumerate(steps):
        target = plane_head(step)
        rows = pl.ds(pl.multiple_of(16 * target, 16), 16)
        sums.append(
            send(rs_out.at[rows], sum_h.at[h], sum_ss.at[i], sum_rs.at[i], (c, target))
        )

    inter = jnp.zeros((HEADS, ROWS), F32)
    end_row = []
    for half in range(2):
        lanes = slice(256 * half, 256 * half + 256)
        state, adjoint = into[0, half], into[1, half]
        state_out = loc[0, half, 0:STATE] + loc[0, half, STATE : STATE + 1] * state
        end_row.append(jnp.sum(adjoint * state_out, axis=0, keepdims=True))
        after_part = wout[:, lanes] * dot(bp[...], adjoint.astype(BF16))
        before_part = win[:, lanes] * dot(cp[...], state.astype(BF16))
        pg[0:ROWS, lanes] = (agr[:, lanes] + after_part) * slope[:, lanes]
        difference = before_part * gr[:, lanes].astype(F32) - after_part * act[:, lanes].astype(F32)
        inter = inter + exact_dot(pick[:, lanes], difference, NT)
    hb_s[...] = pg[0:8] * keep_in[0:8]
    back = send(hb_s, hb_r, halo_ss.at[1], halo_rs.at[1], before)

    ends = jnp.sum(pick * jnp.concatenate(end_row, axis=1), axis=1, keepdims=True)
    cum_total = rowtot[...] + inter - xcol[...].T[0:HEADS]
    o_dec[...] = exact_dot(cum_total, lower) + ends
    stores = [pltpu.make_async_copy(o_dec, dec_h, store.at[5])]
    stores[0].start()

    back.wait_recv()
    is_last = (c < total - 1).astype(F32)
    pg[ROWS:] = hb_r[...] * is_last
    for chunk in range(4):
        lanes = slice(128 * chunk, 128 * chunk + 128)
        value = cw[0:1, lanes] * pg[0:ROWS, lanes]
        for k in range(1, TAPS):
            valid = (cnt[8 + k : 8 + k + ROWS] == cnt[8 : 8 + ROWS]).astype(F32)
            value = value + cw[k : k + 1, lanes] * pg[k : k + ROWS, lanes] * valid
        o_in[:, lanes] = value
        stores.append(pltpu.make_async_copy(o_in.at[:, lanes], in_h.at[:, lanes], store.at[chunk]))
        stores[-1].start()

    for copy in sums:
        copy.wait_recv()
    stores.append(keep)
    for copy in stores:
        copy.wait()

    for copy in sends:
        copy.wait_send()

    @pl.when(middle)
    def _():
        relay.wait_send()

    @pl.when(upper_half)
    def _():
        direct.wait_send()


def finish(a_in, a_sum, a_dec, o_in, o_b, o_c, o_dec, wide, sums, both, decay, load, store):
    def go(i, src, dst, sem):
        return pltpu.make_async_copy(src, dst, sem.at[i])

    half = ROWS // 2
    triples = [(a_sum, sums, None)]
    triples += [(a_in.at[p], wide.at[p], o_in.at[p]) for p in (pl.ds(0, half), pl.ds(half, half))]
    triples += [(a_dec, decay, o_dec)]
    loads = [go(i, src, mid, load) for i, (src, mid, _) in enumerate(triples)]
    stores = [go(0, both.at[0], o_b, store)]
    stores += [go(i, mid, dst, store) for i, (_, mid, dst) in enumerate(triples) if i > 0]
    stores += [go(4, both.at[1], o_c, store)]
    for copy in loads:
        copy.start()
    for i in range(1, 4):
        loads[i].wait()
        stores[i].start()
    loads[0].wait()
    total = sums[0].astype(F32)
    for j in range(1, sums.shape[0]):
        total = total + sums[j].astype(F32)
    both[0] = total[:, 0:STATE]
    both[1] = total[:, STATE:]
    stores[0].start()
    stores[4].start()
    for copy in stores:
        copy.wait()


def body(tokens_in, starts, log_decay, b_proj, c_proj, out_grad, conv_weight, conv_bias, skip_gain):
    chips = lax.axis_size("ctx") // 2
    planes = lax.axis_size("head")
    groups = chips // CUBE
    own = ROWS // planes
    vmem = pltpu.VMEM
    dma = pltpu.SemaphoreType.DMA
    in_grad, sums, decay_grad = pl.pallas_call(
        functools.partial(kernel, chips, planes),
        out_shape=(
            jax.ShapeDtypeStruct((ROWS, WIDE), F32),
            jax.ShapeDtypeStruct((planes, own, 2 * STATE), BF16),
            jax.ShapeDtypeStruct((HEADS, ROWS), F32),
        ),
        in_specs=[pl.BlockSpec(memory_space=pltpu.HBM)] * 9,
        out_specs=[pl.BlockSpec(memory_space=pltpu.HBM)] * 3,
        scratch_shapes=[
            vmem((ROWS, WIDE), F32),
            vmem((HEADS, ROWS), F32),
            vmem((ROWS, WIDE), BF16),
            vmem((1, ROWS), jnp.int32),
            vmem((HEADS, ROWS), F32),
            vmem((ROWS, STATE), BF16),
            vmem((ROWS, STATE), BF16),
            vmem((ROWS, WIDE), BF16),
            vmem((TAPS, WIDE), F32),
            vmem((1, WIDE), F32),
            vmem((1, HEADS), F32),
            vmem((8 + ROWS, WIDE), F32),
            vmem((16 + ROWS, 128), F32),
            vmem((2 * HEADS, ROWS), F32),
            vmem((ROWS, WIDE), BF16),
            vmem((ROWS, WIDE), F32),
            vmem((2, ROWS, WIDE), BF16),
            vmem((2, ROWS, WIDE), BF16),
            vmem((ROWS, WIDE), F32),
            vmem((ROWS, WIDE), F32),
            vmem((ROWS, WIDE), F32),
            vmem((ROWS, ROWS), F32),
            vmem((HEADS, ROWS), F32),
            vmem((ROWS, 128), F32),
            vmem((2, 2, STATE + 8, 256), F32),
            vmem((2, STATE + 8, 256), F32),
            vmem((STATE + 8, 256), F32),
            vmem((CUBE, 144, 128), jnp.int16),
            vmem((CUBE, 144, 128), jnp.int16),
            vmem((2, 80, 128), jnp.int16),
            vmem((groups, 80, 128), jnp.int16),
            vmem((CUBE, 144, 128), jnp.int16),
            vmem((2, CUBE, 144, 128), jnp.int16),
            vmem((2, 2, STATE, 256), F32),
            vmem((ROWS, 2 * STATE), F32),
            vmem((ROWS, 2 * STATE), BF16),
            vmem((16, WIDE), BF16),
            vmem((16, WIDE), BF16),
            vmem((8, WIDE), F32),
            vmem((8, WIDE), F32),
            vmem((8 + ROWS, WIDE), F32),
            dma((3,)),
            dma((3,)),
            dma((2,)),
            dma((2,)),
            dma((CUBE - 1,)),
            dma((CUBE - 1,)),
            dma((4,)),
            dma((3,)),
            dma((CUBE - 1,)),
            dma((CUBE - 1,)),
            dma((CUBE,)),
            dma((CUBE,)),
            dma((max(planes - 1, 1),)),
            dma((max(planes - 1, 1),)),
            pltpu.SemaphoreType.REGULAR,
            pltpu.SemaphoreType.REGULAR,
            pltpu.SemaphoreType.REGULAR,
            pltpu.SemaphoreType.REGULAR,
            dma((9,)),
            dma((6,)),
        ],
        compiler_params=pltpu.CompilerParams(
            collective_id=0, has_side_effects=True, vmem_limit_bytes=63 * 1024 * 1024
        ),
        name="layer",
    )(
        tokens_in,
        starts.reshape(1, ROWS),
        log_decay,
        b_proj,
        c_proj,
        out_grad,
        conv_weight,
        conv_bias.reshape(1, WIDE),
        skip_gain.reshape(1, HEADS),
    )
    in_grad, b_grad, c_grad, decay_grad = pl.pallas_call(
        finish,
        out_shape=(
            jax.ShapeDtypeStruct((ROWS, WIDE), F32),
            jax.ShapeDtypeStruct((own, STATE), F32),
            jax.ShapeDtypeStruct((own, STATE), F32),
            jax.ShapeDtypeStruct((HEADS, ROWS), F32),
        ),
        in_specs=[pl.BlockSpec(memory_space=pl.ANY)] * 3,
        out_specs=[pl.BlockSpec(memory_space=pltpu.HBM)] * 4,
        scratch_shapes=[
            vmem((ROWS, WIDE), F32),
            vmem((planes, own, 2 * STATE), BF16),
            vmem((2, own, STATE), F32),
            vmem((HEADS, ROWS), F32),
            dma((4,)),
            dma((5,)),
        ],
        compiler_params=pltpu.CompilerParams(vmem_limit_bytes=63 * 1024 * 1024),
        name="finish",
    )(in_grad, sums, decay_grad)
    return (in_grad, b_grad, c_grad, decay_grad)


def solution(mesh):
    placed = (
        P("ctx", "head"),
        P("ctx"),
        P("head", "ctx"),
        P("ctx", None),
        P("ctx", None),
        P("ctx", "head"),
        P(None, "head"),
        P("head"),
        P("head"),
    )
    return jax.shard_map(
        body,
        mesh=mesh,
        in_specs=placed,
        out_specs=(
            P("ctx", "head"),
            P(("ctx", "head"), None),
            P(("ctx", "head"), None),
            P("head", "ctx"),
        ),
        check_vma=False,
    )
```

```python
import functools
import math

import jax
import jax.numpy as jnp
from jax import lax
from jax.experimental import pallas as pl
from jax.experimental.pallas import tpu as pltpu
from jax.sharding import PartitionSpec as P

MESH = pl.DeviceIdType.MESH
F32 = jnp.float32
BF16 = jnp.bfloat16
HIGHEST = lax.Precision.HIGHEST

ROWS = 256
HEADS = 8
WIDE = 512
STATE = 128
TAPS = 4
CUBE = 4

NN = (((1,), (0,)), ((), ()))
NT = (((1,), (1,)), ((), ()))
TN = (((0,), (0,)), ((), ()))


def dot(a, b, dims=NN):
    return lax.dot_general(a, b, dims, preferred_element_type=F32)


def exact_dot(a, b, dims=NN):
    return lax.dot_general(a, b, dims, precision=HIGHEST, preferred_element_type=F32)


def split(x):
    high = x.astype(BF16)
    return high, (x - high.astype(F32)).astype(BF16)


def sum_dot(x, ones, dims=NN, first=True):
    high = x.astype(BF16)
    rest = x - high.astype(F32)
    middle = rest.astype(BF16)
    low = (rest - middle.astype(F32)).astype(BF16)
    parts = [dot(p, ones, dims) if first else dot(ones, p, dims) for p in (high, middle, low)]
    return parts[0] + (parts[1] + parts[2])


def wide_dot(x, y, dims=NN):
    high, low = split(x)
    return dot(high, y, dims) + dot(low, y, dims)


def scale_of(exponent):
    return jnp.exp2(exponent.astype(F32))


def exponent_of(largest):
    bits = jnp.floor(jnp.log(jnp.maximum(largest, 1e-36)) * 1.4426950408889634) + 1.0
    return jnp.clip(bits, -100.0, 100.0)


def code(x, exponent):
    return jnp.floor(x * scale_of(14.0 - exponent) + 0.5).astype(jnp.int32)


def pack(x):
    exponent = exponent_of(jnp.max(jnp.abs(x), axis=0, keepdims=True))
    return code(x, exponent).astype(jnp.int16), exponent


def pack_row(x):
    exponent = exponent_of(x)
    return code(x, exponent).astype(F32), exponent


def unpack(x, exponent):
    return x.astype(jnp.int32).astype(F32) * scale_of(exponent - 14.0)


def tile_of(*rows):
    row_of = lax.broadcasted_iota(jnp.int32, (16, 128), 0)
    tile = jnp.zeros((16, 128), F32)
    for i, row in enumerate(rows):
        tile = jnp.where(row_of == i, row, tile)
    return tile.astype(jnp.int32).astype(jnp.int16)


def block_of(place):
    row, lane = 64 * (place // 2), 128 * (place % 2)
    return slice(row, row + 64), slice(lane, lane + 128)


def kernel(
    chips,
    planes,
    tok_h,
    sta_h,
    log_h,
    bp_h,
    cp_h,
    gr_h,
    cw_h,
    cb_h,
    gain_h,
    in_h,
    sum_h,
    dec_h,
    o_in,
    o_dec,
    tok,
    sta,
    log,
    bp,
    cp,
    gr,
    cw,
    cb,
    gain,
    ext,
    cnt,
    stk,
    act,
    slope,
    wact,
    wgr,
    win,
    wout,
    agr,
    sg,
    rowtot,
    xcol,
    loc,
    rx_full,
    rx_half,
    chip,
    l1,
    out2,
    l2,
    o3,
    full,
    into,
    rs_src,
    rs_out,
    halo_s,
    halo_r,
    hb_s,
    hb_r,
    pg,
    pair_ss,
    pair_rs,
    halo_ss,
    halo_rs,
    l1_ss,
    l1_rs,
    l2_ss,
    l2_rs,
    l3_ss,
    l3_rs,
    fw_ss,
    fw_rs,
    sum_ss,
    sum_rs,
    row_ready,
    edge_ready,
    cube_ready,
    far_ready,
    load,
    store,
):
    groups = chips // CUBE
    side = math.isqrt(planes)
    total = 2 * chips
    c = lax.axis_index("ctx")
    h = lax.axis_index("head")
    core = lax.rem(c, 2)
    other = 1 - core
    z = lax.div(c, 2)
    group = lax.div(z, CUBE)
    place = lax.rem(z, CUBE)
    after = (lax.rem(c + 1, total), h)
    before = (lax.rem(c + total - 1, total), h)
    partner = (2 * z + other, h)

    def in_cube(d):
        return lax.rem(place + d, CUBE)

    def cube_device(d):
        return (2 * (CUBE * group + in_cube(d)) + core, h)

    def other_group(d):
        return lax.rem(group + d, groups)

    def group_device(d):
        return (2 * (CUBE * other_group(d) + place) + core, h)

    def along(d):
        return lax.div(h, side) * side + lax.rem(lax.rem(h, side) + d, side)

    def across(d):
        return lax.rem(h + side * d, planes)

    steps = [(dx, dy) for dx in range(side) for dy in range(side) if dx + dy > 0]
    steps.sort(key=lambda step: -sum(min(d, side - d) for d in step))

    def plane_head(step):
        row = lax.rem(lax.div(h, side) + step[0], side)
        return side * row + lax.rem(lax.rem(h, side) + step[1], side)

    def chip_device(d):
        return (2 * lax.rem(z + d + chips, chips) + core, h)

    barrier = pltpu.get_barrier_semaphore()
    peers = [after, before, chip_device(1), chip_device(-1)]
    peers += [cube_device(d) for d in range(1, CUBE)]
    peers += [(c, along(d)) for d in range(1, side)]
    peers += [(c, across(d)) for d in range(1, side)]
    for peer in peers:
        pl.semaphore_signal(barrier, inc=1, device_id=peer, device_id_type=MESH)

    pairs = (
        (sta_h, sta),
        (log_h, log),
        (cp_h, cp),
        (gr_h, gr),
        (tok_h, tok),
        (cw_h, cw),
        (cb_h, cb),
        (bp_h, bp),
        (gain_h, gain),
    )
    loads = [
        pltpu.make_async_copy(src, dst, load.at[i]) for i, (src, dst) in enumerate(pairs)
    ]
    for copy in loads:
        copy.start()
    sends = []

    def send(src, dst, send_sem, recv_sem, device, now=True):
        copy = pltpu.make_async_remote_copy(
            src_ref=src,
            dst_ref=dst,
            send_sem=send_sem,
            recv_sem=recv_sem,
            device_id=device,
            device_id_type=MESH,
        )
        if now:
            copy.start()
        sends.append(copy)
        return copy

    loads[0].wait()
    loads[1].wait()
    i0 = lax.broadcasted_iota(jnp.int32, (ROWS, ROWS), 0)
    i1 = lax.broadcasted_iota(jnp.int32, (ROWS, ROWS), 1)
    upper = (i0 <= i1).astype(F32)
    lower = (i0 >= i1).astype(F32)
    stk[0:HEADS] = log[...]
    stk[HEADS : 2 * HEADS] = jnp.broadcast_to(sta[...].astype(F32), (HEADS, ROWS))
    cum_row = sum_dot(stk[...], upper.astype(BF16))
    cum_col = sum_dot(stk[...], lower.astype(BF16), NT, first=False)
    cnt_row = cum_row[HEADS : HEADS + 1]
    cnt_col = cum_col[:, HEADS : HEADS + 1]
    cnt_last = cnt_col[ROWS - 1 : ROWS]
    log_col = cum_col[:, 0:HEADS]
    keep_in = (cnt_col == 0.0).astype(F32)
    keep_out = (cnt_col == cnt_last).astype(F32)
    cnt[0:8] = jnp.zeros((8, 128), F32)
    cnt[8 : 8 + ROWS] = jnp.broadcast_to(cnt_col, (ROWS, 128))
    cnt[8 + ROWS : 16 + ROWS] = jnp.broadcast_to(cnt_last, (8, 128))
    head_of = lax.broadcasted_iota(jnp.int32, (HEADS, WIDE), 0)
    lane_of = lax.broadcasted_iota(jnp.int32, (HEADS, WIDE), 1)
    pick = (lax.div(lane_of, WIDE // HEADS) == head_of).astype(F32)
    picked = pick.astype(BF16)
    win[...] = wide_dot(jnp.exp(log_col) * keep_in, picked)
    wout[...] = wide_dot(jnp.exp(log_col[ROWS - 1 : ROWS] - log_col) * keep_out, picked)
    factor = win[ROWS - 1 : ROWS, :]
    for half in range(2):
        lanes = slice(256 * half, 256 * half + 256)
        for which in range(2):
            loc[which, half, STATE : STATE + 8] = jnp.broadcast_to(factor[:, lanes], (8, 256))

    loads[2].wait()
    loads[3].wait()
    for half in range(2):
        lanes = slice(256 * half, 256 * half + 256)
        high, low = split(win[:, lanes] * gr[:, lanes].astype(F32))
        wgr[0, :, lanes] = high
        wgr[1, :, lanes] = low
        loc[1, half, 0:STATE] = dot(cp[...], high, TN) + dot(cp[...], low, TN)

    for copy in loads[4:]:
        copy.wait()
    halo_s[...] = tok[ROWS - 16 :] * keep_out[ROWS - 16 :].astype(BF16)

    def convolve(first, rows):
        for chunk in range(4):
            lanes = slice(128 * chunk, 128 * chunk + 128)
            here = cnt[8 + first : 8 + first + rows]
            value = cb[:, lanes] + cw[0:1, lanes] * ext[8 + first : 8 + first + rows, lanes]
            for k in range(1, TAPS):
                rows_at = slice(8 - k + first, 8 - k + first + rows)
                valid = (here == cnt[rows_at]).astype(F32)
                value = value + cw[k : k + 1, lanes] * ext[rows_at, lanes] * valid
            sigma = 1.0 / (1.0 + jnp.exp(-value))
            act[first : first + rows, lanes] = (value * sigma).astype(BF16)
            slope[first : first + rows, lanes] = sigma * (1.0 + value * (1.0 - sigma))

    ext[0:8] = jnp.zeros((8, WIDE), F32)
    ext[8:] = tok[...].astype(F32)
    convolve(0, ROWS)

    def local_state(rows, half):
        lanes = slice(256 * half, 256 * half + 256)
        high, low = split(wout[rows, lanes] * act[rows, lanes].astype(F32))
        wact[0, rows, lanes] = high
        wact[1, rows, lanes] = low
        return dot(bp[rows], high, TN) + dot(bp[rows], low, TN)

    for half in range(2):
        loc[0, half, 0:STATE] = local_state(slice(16, ROWS), half)

    pl.semaphore_wait(barrier, len(peers))
    halo = send(halo_s, halo_r, halo_ss.at[0], halo_rs.at[0], after)
    first = send(
        loc.at[core, other], rx_full.at[other], pair_ss.at[0], pair_rs.at[0], partner, now=False
    )
    second = send(
        loc.at[other, other], rx_half, pair_ss.at[1], pair_rs.at[1], partner, now=False
    )

    @pl.when(core == 1)
    def _():
        first.start()

    @pl.when(core == 0)
    def _():
        second.start()

    lowest, highest = place == 0, place == CUBE - 1
    for d in range(1, side):
        pl.semaphore_signal(row_ready, inc=1, device_id=(c, across(d)), device_id_type=MESH)
    for edge, d in ((lowest, -1), (highest, 1)):

        @pl.when(edge)
        def _():
            pl.semaphore_signal(edge_ready, inc=1, device_id=chip_device(d), device_id_type=MESH)

    halo.wait_recv()
    is_first = (c > 0).astype(F32)
    ext[0:8] = halo_r[8:16].astype(F32) * is_first
    convolve(0, 16)

    for half in range(2):
        loc[0, half, 0:STATE] += local_state(slice(0, 16), half)

    @pl.when(core == 0)
    def _():
        first.start()

    @pl.when(core == 1)
    def _():
        second.start()

    third = send(loc.at[core, core], rx_full.at[core], pair_ss.at[2], pair_rs.at[2], partner)

    @pl.when(lowest | highest)
    def _():
        pl.semaphore_wait(edge_ready, 1)
        for d in range(1, CUBE):
            pl.semaphore_signal(
                cube_ready, inc=1, device_id=cube_device(d), device_id_type=MESH
            )

    first.wait_recv()
    second.wait_recv()
    f_own = loc[0, core, STATE : STATE + 1]
    f_other = rx_half[STATE : STATE + 1]
    is_late = core == 1
    factor_code, factor_exponent = pack_row(f_own * f_other)
    for s in range(CUBE):
        rows, lanes = block_of(s)
        mine, e_mine = pack(rx_half[rows, lanes] + f_other[:, lanes] * loc[core, core, rows, lanes])
        yours, e_yours = pack(
            loc[other, core, rows, lanes] + f_own[:, lanes] * rx_full[core, rows, lanes]
        )
        chip[s, pl.ds(pl.multiple_of(64 * core, 64), 64)] = mine
        chip[s, pl.ds(pl.multiple_of(64 * other, 64), 64)] = yours
        chip[s, 128:144] = tile_of(
            jnp.where(is_late, e_yours, e_mine),
            jnp.where(is_late, e_mine, e_yours),
            factor_exponent[:, lanes],
            factor_code[:, lanes],
        )

    l1[place] = chip[place]
    ups = []
    for d in range(1, CUBE):
        ups.append(
            send(chip.at[in_cube(d)], l1.at[place], l1_ss.at[d - 1], l1_rs.at[d - 1], cube_device(d))
        )

    inside = jnp.logical_not(lowest | highest)
    middle = (group > 0) & (group < groups - 1)
    upper_half = group >= 2
    pl.semaphore_wait(cube_ready, 1 + inside.astype(jnp.int32))

    @pl.when(middle)
    def _():
        pl.semaphore_signal(far_ready, inc=1, device_id=group_device(1), device_id_type=MESH)

    gain_wide = exact_dot(jnp.broadcast_to(gain[...], (8, HEADS)), pick)[0:1]
    scores = dot(bp[...], cp[...], NT)
    bias = jnp.where((i0 <= i1) & (cnt_col == cnt_row), 0.0, -1e30)
    even = lax.broadcasted_iota(jnp.int32, (ROWS, 128), 1) < 64

    def intra(pair, begin):
        lanes = slice(128 * pair, 128 * pair + 128)
        parts = []
        for head in (2 * pair, 2 * pair + 1):
            decay = jnp.exp(cum_row[head : head + 1] - cum_col[:, head : head + 1] + bias)
            mixed = decay * scores
            parts.append(dot(mixed.astype(BF16), gr[:, lanes]))
            mine = even if head % 2 == 0 else ~even
            rows = jnp.where(mine, act[:, lanes].astype(F32), 0.0).astype(BF16)
            inner = dot(rows, gr[:, lanes], NT)
            if begin and head % 2 == 0:
                sg[...] = decay * inner
            else:
                sg[...] += decay * inner
            product = mixed * inner
            rowtot[head : head + 1] = jnp.sum(product, axis=0, keepdims=True)
            xcol[:, head : head + 1] = jnp.sum(product, axis=1, keepdims=True)
        agr[:, lanes] = jnp.where(even, parts[0], parts[1]) + gain_wide[:, lanes] * gr[
            :, lanes
        ].astype(F32)

    intra(0, True)
    intra(1, False)

    for copy in ups:
        copy.wait_recv()

    def unpack_slot(ref, j, arrays):
        tile = ref[j, 64 * arrays : 64 * arrays + 16].astype(jnp.int32).astype(F32)
        values = [
            unpack(ref[j, 64 * i : 64 * i + 64], tile[i : i + 1]) for i in range(arrays)
        ]
        factor = tile[arrays + 1 : arrays + 2] * scale_of(tile[arrays : arrays + 1] - 14.0)
        return values, factor

    slots = [unpack_slot(l1, j, 2) for j in range(CUBE)]

    def prefixes():
        values, factors = [jnp.zeros((64, 128), F32)], [jnp.ones((1, 128), F32)]
        for (state, _), f in slots:
            values.append(state + f * values[-1])
            factors.append(f * factors[-1])
        return values, factors

    def suffixes():
        values, factors = [jnp.zeros((64, 128), F32)], [jnp.ones((1, 128), F32)]
        for (_, adjoint), f in reversed(slots):
            values.append(adjoint + f * values[-1])
            factors.append(f * factors[-1])
        return values[::-1], factors[::-1]

    down, down_f = prefixes()
    up, up_f = suffixes()
    factor_code, factor_exponent = pack_row(down_f[CUBE])
    for kind, total_here in enumerate((down[CUBE], up[0])):
        coded, exponent = pack(total_here)
        out2[kind, 0:64] = coded
        out2[kind, 64:80] = tile_of(exponent, factor_exponent, factor_code)
    crosses = []
    for i, d in enumerate((1, groups - 1)):
        kind = (other_group(d) < group).astype(jnp.int32)
        crosses.append(
            send(out2.at[kind], l2.at[group], l2_ss.at[i], l2_rs.at[i], group_device(d))
        )

    def to_group(src, slot, i, d):
        return pltpu.make_async_remote_copy(
            src_ref=src,
            dst_ref=l2.at[slot],
            send_sem=l2_ss.at[i],
            recv_sem=l2_rs.at[2],
            device_id=group_device(d),
            device_id_type=MESH,
        )

    relay = to_group(l2.at[other_group(groups - 1)], other_group(groups - 1), 2, 1)
    direct = to_group(out2.at[1], group, 3, 2)

    @pl.when(upper_half)
    def _():
        pl.semaphore_wait(far_ready, 1)
        direct.start()

    intra(2, False)
    intra(3, False)

    crosses[0].wait_recv()

    @pl.when(middle)
    def _():
        relay.start()

    crosses[1].wait_recv()
    relay.wait_recv()
    totals = [unpack_slot(l2, u, 1) for u in range(groups)]
    from_before = jnp.zeros((64, 128), F32)
    for u in range(groups):
        (value,), f = totals[u]
        from_before = jnp.where(u < group, value + f * from_before, from_before)
    from_after = jnp.zeros((64, 128), F32)
    for u in reversed(range(groups)):
        (value,), f = totals[u]
        from_after = jnp.where(u > group, value + f * from_after, from_after)
    for j in range(CUBE):
        state, e_state = pack(down[j] + down_f[j] * from_before)
        adjoint, e_adjoint = pack(up[j + 1] + up_f[j + 1] * from_after)
        o3[j, 0:64] = state
        o3[j, 64:128] = adjoint
        o3[j, 128:144] = tile_of(e_state, e_adjoint)
    full[core, place] = o3[place]
    forwards = []
    backs = []
    for d in range(1, CUBE):
        backs.append(
            send(
                o3.at[in_cube(d)],
                full.at[core, place],
                l3_ss.at[d - 1],
                l3_rs.at[d - 1],
                cube_device(d),
            )
        )
    here = full.at[core, place]
    forwards.append(send(here, here, fw_ss.at[0], fw_rs.at[0], partner))

    high, low = split(sg[...])
    rs_src[:, 0:STATE] = dot(high, cp[...]) + dot(low, cp[...])
    rs_src[:, STATE:] = dot(high, bp[...], TN) + dot(low, bp[...], TN)

    for d in range(1, CUBE):
        backs[d - 1].wait_recv()
        slot = full.at[core, in_cube(CUBE - d)]
        forwards.append(send(slot, slot, fw_ss.at[d], fw_rs.at[d], partner))
    third.wait_recv()

    def incoming(half, which):
        blocks = []
        for s in range(CUBE):
            tile = full[half, s, 128:144].astype(jnp.int32).astype(F32)
            blocks.append(
                unpack(full[half, s, 64 * which : 64 * which + 64], tile[which : which + 1])
            )
        top = jnp.concatenate(blocks[0:2], axis=1)
        return jnp.concatenate([top, jnp.concatenate(blocks[2:4], axis=1)], axis=0)

    late = (core == 1).astype(F32)
    early = 1.0 - late

    for half in (core, other):
        if half is other:
            for copy in forwards:
                copy.wait_recv()
        lanes = pl.ds(pl.multiple_of(256 * half, 256), 256)
        f_other = rx_full[half, STATE : STATE + 1]
        received = rx_full[half, 0:STATE]
        state = late * received + (late * f_other + early) * incoming(half, 0)
        adjoint = early * received + (early * f_other + late) * incoming(half, 1)
        into[0, half] = state
        into[1, half] = adjoint
        for which, value, rows in ((0, adjoint, wact), (1, state, wgr)):
            high, low = split(value)
            both = dot(rows[0, :, lanes], jnp.concatenate([high, low], axis=0), NT)
            part = both[:, 0:STATE] + both[:, STATE:] + dot(rows[1, :, lanes], high, NT)
            columns = slice(STATE * which, STATE * which + STATE)
            if half is other:
                rs_out[:, columns] = (rs_src[:, columns] + part).astype(BF16)
            else:
                rs_src[:, columns] += part

    keep = pltpu.make_async_copy(
        rs_out.at[pl.ds(pl.multiple_of(16 * h, 16), 16)], sum_h.at[h], store.at[4]
    )
    keep.start()
    pl.semaphore_wait(row_ready, side - 1)
    sums = []
    for i, step in enumerate(steps):
        target = plane_head(step)
        rows = pl.ds(pl.multiple_of(16 * target, 16), 16)
        sums.append(
            send(rs_out.at[rows], sum_h.at[h], sum_ss.at[i], sum_rs.at[i], (c, target))
        )

    inter = jnp.zeros((HEADS, ROWS), F32)
    end_row = []
    for half in range(2):
        lanes = slice(256 * half, 256 * half + 256)
        state, adjoint = into[0, half], into[1, half]
        state_out = loc[0, half, 0:STATE] + loc[0, half, STATE : STATE + 1] * state
        end_row.append(jnp.sum(adjoint * state_out, axis=0, keepdims=True))
        after_part = wout[:, lanes] * dot(bp[...], adjoint.astype(BF16))
        before_part = win[:, lanes] * dot(cp[...], state.astype(BF16))
        pg[0:ROWS, lanes] = (agr[:, lanes] + after_part) * slope[:, lanes]
        difference = before_part * gr[:, lanes].astype(F32) - after_part * act[:, lanes].astype(F32)
        inter = inter + exact_dot(pick[:, lanes], difference, NT)
    hb_s[...] = pg[0:8] * keep_in[0:8]
    back = send(hb_s, hb_r, halo_ss.at[1], halo_rs.at[1], before)

    ends = jnp.sum(pick * jnp.concatenate(end_row, axis=1), axis=1, keepdims=True)
    cum_total = rowtot[...] + inter - xcol[...].T[0:HEADS]
    o_dec[...] = exact_dot(cum_total, lower) + ends
    stores = [pltpu.make_async_copy(o_dec, dec_h, store.at[5])]
    stores[0].start()

    back.wait_recv()
    is_last = (c < total - 1).astype(F32)
    pg[ROWS:] = hb_r[...] * is_last
    for chunk in range(4):
        lanes = slice(128 * chunk, 128 * chunk + 128)
        value = cw[0:1, lanes] * pg[0:ROWS, lanes]
        for k in range(1, TAPS):
            valid = (cnt[8 + k : 8 + k + ROWS] == cnt[8 : 8 + ROWS]).astype(F32)
            value = value + cw[k : k + 1, lanes] * pg[k : k + ROWS, lanes] * valid
        o_in[:, lanes] = value
        stores.append(pltpu.make_async_copy(o_in.at[:, lanes], in_h.at[:, lanes], store.at[chunk]))
        stores[-1].start()

    for copy in sums:
        copy.wait_recv()
    stores.append(keep)
    for copy in stores:
        copy.wait()

    for copy in sends:
        copy.wait_send()

    @pl.when(middle)
    def _():
        relay.wait_send()

    @pl.when(upper_half)
    def _():
        direct.wait_send()


def finish(a_in, a_sum, a_dec, o_in, o_b, o_c, o_dec, wide, sums, both, decay, load, store):
    def go(i, src, dst, sem):
        return pltpu.make_async_copy(src, dst, sem.at[i])

    half = ROWS // 2
    triples = [(a_sum, sums, None)]
    triples += [(a_in.at[p], wide.at[p], o_in.at[p]) for p in (pl.ds(0, half), pl.ds(half, half))]
    triples += [(a_dec, decay, o_dec)]
    loads = [go(i, src, mid, load) for i, (src, mid, _) in enumerate(triples)]
    stores = [go(0, both.at[0], o_b, store)]
    stores += [go(i, mid, dst, store) for i, (_, mid, dst) in enumerate(triples) if i > 0]
    stores += [go(4, both.at[1], o_c, store)]
    for copy in loads:
        copy.start()
    for i in range(1, 4):
        loads[i].wait()
        stores[i].start()
    loads[0].wait()
    total = sums[0].astype(F32)
    for j in range(1, sums.shape[0]):
        total = total + sums[j].astype(F32)
    both[0] = total[:, 0:STATE]
    both[1] = total[:, STATE:]
    stores[0].start()
    stores[4].start()
    for copy in stores:
        copy.wait()


def body(tokens_in, starts, log_decay, b_proj, c_proj, out_grad, conv_weight, conv_bias, skip_gain):
    chips = lax.axis_size("ctx") // 2
    planes = lax.axis_size("head")
    groups = chips // CUBE
    own = ROWS // planes
    vmem = pltpu.VMEM
    dma = pltpu.SemaphoreType.DMA
    in_grad, sums, decay_grad = pl.pallas_call(
        functools.partial(kernel, chips, planes),
        out_shape=(
            jax.ShapeDtypeStruct((ROWS, WIDE), F32),
            jax.ShapeDtypeStruct((planes, own, 2 * STATE), BF16),
            jax.ShapeDtypeStruct((HEADS, ROWS), F32),
        ),
        in_specs=[pl.BlockSpec(memory_space=pltpu.HBM)] * 9,
        out_specs=[pl.BlockSpec(memory_space=pltpu.HBM)] * 3,
        scratch_shapes=[
            vmem((ROWS, WIDE), F32),
            vmem((HEADS, ROWS), F32),
            vmem((ROWS, WIDE), BF16),
            vmem((1, ROWS), jnp.int32),
            vmem((HEADS, ROWS), F32),
            vmem((ROWS, STATE), BF16),
            vmem((ROWS, STATE), BF16),
            vmem((ROWS, WIDE), BF16),
            vmem((TAPS, WIDE), F32),
            vmem((1, WIDE), F32),
            vmem((1, HEADS), F32),
            vmem((8 + ROWS, WIDE), F32),
            vmem((16 + ROWS, 128), F32),
            vmem((2 * HEADS, ROWS), F32),
            vmem((ROWS, WIDE), BF16),
            vmem((ROWS, WIDE), F32),
            vmem((2, ROWS, WIDE), BF16),
            vmem((2, ROWS, WIDE), BF16),
            vmem((ROWS, WIDE), F32),
            vmem((ROWS, WIDE), F32),
            vmem((ROWS, WIDE), F32),
            vmem((ROWS, ROWS), F32),
            vmem((HEADS, ROWS), F32),
            vmem((ROWS, 128), F32),
            vmem((2, 2, STATE + 8, 256), F32),
            vmem((2, STATE + 8, 256), F32),
            vmem((STATE + 8, 256), F32),
            vmem((CUBE, 144, 128), jnp.int16),
            vmem((CUBE, 144, 128), jnp.int16),
            vmem((2, 80, 128), jnp.int16),
            vmem((groups, 80, 128), jnp.int16),
            vmem((CUBE, 144, 128), jnp.int16),
            vmem((2, CUBE, 144, 128), jnp.int16),
            vmem((2, 2, STATE, 256), F32),
            vmem((ROWS, 2 * STATE), F32),
            vmem((ROWS, 2 * STATE), BF16),
            vmem((16, WIDE), BF16),
            vmem((16, WIDE), BF16),
            vmem((8, WIDE), F32),
            vmem((8, WIDE), F32),
            vmem((8 + ROWS, WIDE), F32),
            dma((3,)),
            dma((3,)),
            dma((2,)),
            dma((2,)),
            dma((CUBE - 1,)),
            dma((CUBE - 1,)),
            dma((4,)),
            dma((3,)),
            dma((CUBE - 1,)),
            dma((CUBE - 1,)),
            dma((CUBE,)),
            dma((CUBE,)),
            dma((max(planes - 1, 1),)),
            dma((max(planes - 1, 1),)),
            pltpu.SemaphoreType.REGULAR,
            pltpu.SemaphoreType.REGULAR,
            pltpu.SemaphoreType.REGULAR,
            pltpu.SemaphoreType.REGULAR,
            dma((9,)),
            dma((6,)),
        ],
        compiler_params=pltpu.CompilerParams(
            collective_id=0, has_side_effects=True, vmem_limit_bytes=63 * 1024 * 1024
        ),
        name="layer",
    )(
        tokens_in,
        starts.reshape(1, ROWS),
        log_decay,
        b_proj,
        c_proj,
        out_grad,
        conv_weight,
        conv_bias.reshape(1, WIDE),
        skip_gain.reshape(1, HEADS),
    )
    in_grad, b_grad, c_grad, decay_grad = pl.pallas_call(
        finish,
        out_shape=(
            jax.ShapeDtypeStruct((ROWS, WIDE), F32),
            jax.ShapeDtypeStruct((own, STATE), F32),
            jax.ShapeDtypeStruct((own, STATE), F32),
            jax.ShapeDtypeStruct((HEADS, ROWS), F32),
        ),
        in_specs=[pl.BlockSpec(memory_space=pl.ANY)] * 3,
        out_specs=[pl.BlockSpec(memory_space=pltpu.HBM)] * 4,
        scratch_shapes=[
            vmem((ROWS, WIDE), F32),
            vmem((planes, own, 2 * STATE), BF16),
            vmem((2, own, STATE), F32),
            vmem((HEADS, ROWS), F32),
            dma((4,)),
            dma((5,)),
        ],
        compiler_params=pltpu.CompilerParams(vmem_limit_bytes=63 * 1024 * 1024),
        name="finish",
    )(in_grad, sums, decay_grad)
    return (in_grad, b_grad, c_grad, decay_grad)


def solution(mesh):
    placed = (
        P("ctx", "head"),
        P("ctx"),
        P("head", "ctx"),
        P("ctx", None),
        P("ctx", None),
        P("ctx", "head"),
        P(None, "head"),
        P("head"),
        P("head"),
    )
    return jax.shard_map(
        body,
        mesh=mesh,
        in_specs=placed,
        out_specs=(
            P("ctx", "head"),
            P(("ctx", "head"), None),
            P(("ctx", "head"), None),
            P("head", "ctx"),
        ),
        check_vma=False,
    )
```
